128 devices in a mesh: tm: 8 (over x, core), chan: 16 (over y, z).
Axes of the slice: x: 4, y: 4, z: 4, core: 2. Of those that a mesh axis runs over, the one named last changes fastest.
Arguments:
- raw_blocks: bfloat16 [32, 10240, 1024], P('tm', 'chan'), may hold values from -6 to 6
- fir_taps: bfloat16 [128], replicated, may hold values from -0.5 to 0.5
- recorder_channel: int32 [10240], replicated, may hold values from 0 to 10239, as said below
- pairs: int32 [8192, 2], P('chan'), may hold values from 0 to 10239, as said below
Outputs:
- stacks: float32 [8192, 256], P('chan')
The draws below stay inside these ranges and needn't reach their ends.
Inputs may be any that keep to these rules, and one draw needn't show every extreme that they name: `recorder_channel`: A permutation of the channels; each aligned block of 640 recorder rows holds exactly 40 channels of every range of 640 consecutive channels. `pairs`: each aligned block of 512 rows names exactly 32 distinct channels of every range of 640 consecutive channels.
All inputs are finite; a program needn't handle non-finite values.
Results may differ from the reference program's by a relative error of at most 0.0084.
Values may be sent and summed in bfloat16 or wider, within the bound.
A program may use at most 128 MiB of HBM per device.

```python
import jax
import jax.numpy as jnp
from jax import lax

L = 1024
TAPS = 128
NB = 128
SMOOTH = 4
CH_DEV = 640
P_DEV = 512
Q = 32
CH = 10240
NWIN = 32
PAIRS = 8192


def draw_recorder_channel(key, part):
    owners = CH // CH_DEV
    per_group = CH_DEV // owners
    subkeys = jax.random.split(key, owners)
    shuffles = jax.vmap(lambda sub: jax.random.permutation(sub, CH_DEV))(subkeys).astype(jnp.int32)
    channel_ids = shuffles + (jnp.arange(owners, dtype=jnp.int32) * CH_DEV)[:, None]
    blocks = channel_ids.reshape(owners, owners, per_group).transpose(1, 0, 2).reshape(owners, CH_DEV)
    second_keys = jax.random.split(jax.random.fold_in(key, 7), owners)
    mixed = jax.vmap(lambda sub, row_ids: jax.random.permutation(sub, row_ids))(second_keys, blocks)
    return mixed.reshape(CH).astype(jnp.int32)


def owner_pairs(sub):
    owners = CH // CH_DEV
    pool_size = owners * Q
    extra_count = 2 * P_DEV - pool_size
    pick_keys = jax.random.split(jax.random.fold_in(sub, 1), owners)
    chosen = jax.vmap(lambda kk: jax.random.permutation(kk, CH_DEV)[:Q])(pick_keys).astype(jnp.int32)
    channel_pool = (chosen + (jnp.arange(owners, dtype=jnp.int32) * CH_DEV)[:, None]).reshape(pool_size)
    channel_pool = jax.random.permutation(jax.random.fold_in(sub, 2), channel_pool)
    draw_one = jax.random.randint(jax.random.fold_in(sub, 3), (extra_count,), 0, pool_size)
    draw_two = jax.random.randint(jax.random.fold_in(sub, 4), (extra_count,), 0, pool_size)
    extra = channel_pool[jnp.minimum(draw_one, draw_two)]
    endpoints = jnp.concatenate([channel_pool, extra])
    endpoints = jax.random.permutation(jax.random.fold_in(sub, 5), endpoints)
    return endpoints.reshape(P_DEV, 2)


def draw_pairs(key, part):
    owners = CH // CH_DEV
    subkeys = jax.random.split(jax.random.fold_in(key, 11), owners)
    return jax.vmap(owner_pairs)(subkeys).reshape(PAIRS, 2).astype(jnp.int32)


def block_scale(rng, dims, shards, smallest, top_value):
    def one(position, blocks):
        steps = jax.random.uniform(jax.random.fold_in(jax.random.fold_in(rng, 6), position), (blocks,), jnp.float32, smallest / len(shards), top_value / len(shards))
        return jnp.repeat(jnp.exp(steps), dims[position] // blocks).reshape((-1,) + (1,) * (len(dims) - position - 1))

    loudness = one(*shards[0])
    for cut in shards[1:]:
        loudness = loudness * one(*cut)
    return loudness


def noise(rng, dims, spread, reach, cuts=(), held_as=jnp.bfloat16):
    result = spread * jax.random.normal(rng, dims, jnp.float32)
    if cuts:
        result = result * block_scale(rng, dims, cuts, -0.22, 0.18)
    return jnp.clip(result, -reach, reach).astype(held_as)


def setup_inputs(seed: int = 0) -> dict:
    splits = jax.random.split(jax.random.key(seed), 5)
    raw_blocks = noise(splits[0], (NWIN, CH, L), 1.0, 6.0, ((0, 8), (1, 16)))
    fir_taps = noise(splits[1], (TAPS,), TAPS ** -0.5, 0.5)
    recorder_channel = draw_recorder_channel(jax.random.fold_in(splits[4], 71), 0)
    pairs = draw_pairs(jax.random.fold_in(splits[4], 71), 0)
    return dict(raw_blocks=raw_blocks, fir_taps=fir_taps, recorder_channel=recorder_channel, pairs=pairs)


def make_fir(fir_taps, length):
    taps_n = fir_taps.shape[0]
    period = taps_n + length
    padded = jnp.concatenate([fir_taps.astype(jnp.float32), jnp.zeros((length,), jnp.float32)])
    repeated = jnp.tile(padded, length)[:length * (period - 1)].reshape(length, period - 1)[:, :length]
    return repeated.astype(jnp.bfloat16)

def make_table(length, bin_count):
    samples = jnp.arange(length, dtype=jnp.int32)
    freqs = jnp.arange(1, bin_count + 1, dtype=jnp.int32)
    phase_idx = samples[:, None] * freqs[None, :] % length
    angles = phase_idx.astype(jnp.float32) * (2.0 * jnp.pi / length)
    return jnp.concatenate([jnp.cos(angles), -jnp.sin(angles)], axis=1).astype(jnp.bfloat16)

def make_smooth(bin_count, half_width):
    places = jnp.arange(bin_count, dtype=jnp.int32)
    band_mask = (jnp.abs(places[:, None] - places[None, :]) <= half_width).astype(jnp.float32)
    return band_mask / lax.optimization_barrier(jnp.sum(band_mask, axis=0, keepdims=True))

def whiten(spectrum, smoother):
    bin_count = spectrum.shape[-1] // 2
    real_part = spectrum[..., :bin_count]
    imag_part = spectrum[..., bin_count:]
    magnitude = jnp.sqrt(real_part * real_part + imag_part * imag_part)
    smoothed = jnp.dot(magnitude, smoother, precision=lax.Precision.HIGHEST)
    mean_level = lax.optimization_barrier(jnp.mean(magnitude, axis=-1, keepdims=True))
    divisor = smoothed + 0.1 * mean_level + 1e-06
    return (spectrum / jnp.concatenate([divisor, divisor], axis=-1)).astype(jnp.bfloat16)

def cross(left_rows, right_rows):
    bin_count = left_rows.shape[-1] // 2
    left_f = left_rows.astype(jnp.float32)
    right_f = right_rows.astype(jnp.float32)
    left_re, left_im = (left_f[..., :bin_count], left_f[..., bin_count:])
    right_re, right_im = (right_f[..., :bin_count], right_f[..., bin_count:])
    real_out = left_re * right_re + left_im * right_im
    imag_out = left_im * right_re - left_re * right_im
    return jnp.concatenate([real_out, imag_out], axis=-1)

def reference(raw_blocks, fir_taps, recorder_channel, pairs):
    rows_of = jnp.argsort(recorder_channel, stable=True).astype(jnp.int32)
    left_idx = rows_of[pairs[:, 0]]
    right_idx = rows_of[pairs[:, 1]]
    fir_matrix = make_fir(fir_taps, L)
    dft_table = make_table(L, NB)
    smoother = make_smooth(NB, SMOOTH)

    def advance(summed, window_rows):
        filtered = jnp.dot(window_rows, fir_matrix, preferred_element_type=jnp.float32).astype(jnp.bfloat16)
        spectrum = jnp.dot(filtered, dft_table, preferred_element_type=jnp.float32)
        whitened = whiten(spectrum, smoother)
        return (summed + cross(whitened[left_idx], whitened[right_idx]), None)
    summed, _ = lax.scan(advance, jnp.zeros((PAIRS, 2 * NB), jnp.float32), raw_blocks)
    return summed / NWIN
```

```python
import jax
import jax.numpy as jnp
import numpy as np
from jax import lax
from jax.experimental import pallas as pl
from jax.experimental.pallas import tpu as pltpu
from jax.sharding import PartitionSpec as P

NB = 128
SMOOTH = 4
CAP = 64
MESH = pl.DeviceIdType.MESH
F32 = jnp.float32
BF16 = jnp.bfloat16
NT = (((1,), (1,)), ((), ()))


def table_values(length, extra):
    samples = np.arange(length, dtype=np.int64)
    freqs = np.arange(1, NB + 1, dtype=np.int64)
    angles = (samples[:, None] * freqs[None, :] % length).astype(np.float32) * np.float32(2.0 * np.pi / length)
    table = np.concatenate([np.cos(angles), -np.sin(angles)], axis=1)
    return np.concatenate([table, np.zeros((extra, 2 * NB), np.float32)]).astype(BF16)


def band_values():
    places = np.arange(NB)
    band = (np.abs(places[:, None] - places[None, :]) <= SMOOTH).astype(np.float32)
    both = np.concatenate([band, np.ones((NB, NB), np.float32)], axis=1)
    return np.concatenate([both, both]).astype(BF16)


def iota(shape, dim):
    return lax.broadcasted_iota(jnp.int32, shape, dim)


def dot(left, right):
    return jnp.dot(left, right, preferred_element_type=F32)


def dot_nt(left, right):
    return lax.dot_general(left, right, NT, preferred_element_type=F32)


def one(condition):
    return jnp.where(condition, 1.0, 0.0)


def ranks_of(marks):
    row, col = iota((128, 128), 0), iota((128, 128), 1)
    marks = jnp.where(row % 8 < 5, marks, 0.0)
    held = marks.astype(BF16)
    upto = dot(held, one(row <= col).astype(BF16))
    totals = dot(held, jnp.ones((128, 128), BF16))
    before = dot(one((row // 8 == col // 8) & (col < row)).astype(BF16), totals.astype(BF16))
    return jnp.where(marks > 0.0, upto + before - 1.0, -1.0), before


def row_of(ref, first):
    return jnp.concatenate([ref[pl.ds(first + k, 1), :] for k in range(5)], axis=1)


def kernel(
    raw_ref, taps_ref, rec_ref, pairs_ref, table_ref, band_ref, out_ref, flag_ref,
    raw, fold, white, marks_out, marks_in, rank, own_rank, pick, send, recv, slot, take, acc, part, parts, whole,
    load_sem, mark_send, mark_recv, row_send, row_recv, part_send, part_recv, whole_send, whole_recv,
):
    t, c = lax.axis_index("tm"), lax.axis_index("chan")
    windows, rows, length = raw.shape
    groups = 16
    team = 8
    pair_count = out_ref.shape[0]
    share = pair_count // team

    for w in range(windows):
        pltpu.make_async_copy(raw_ref.at[w], raw.at[w], load_sem.at[w]).start()

    def chan_peer(k):
        return (c // 4 + k // 4) % 4 * 4 + (c % 4 + k % 4) % 4

    def chan_from(k):
        return (c // 4 + 4 - k // 4) % 4 * 4 + (c % 4 + 4 - k % 4) % 4

    barrier = pltpu.get_barrier_semaphore()

    def greet_chan(k, _):
        pl.semaphore_signal(barrier, inc=1, device_id=(t, chan_peer(k)), device_id_type=MESH)
        return 0

    def greet_tm(k, _):
        pl.semaphore_signal(barrier, inc=1, device_id=((t + k) % team, c), device_id_type=MESH)
        return 0

    lax.fori_loop(1, groups, greet_chan, 0)
    lax.fori_loop(1, team, greet_tm, 0)

    ends = pairs_ref[...]
    high, low = ends // 128, ends % 128
    place = iota((128, pair_count), 0)
    named = jnp.zeros((128, 128), F32)
    for e in range(2):
        named += dot_nt(
            one(low[e : e + 1] == place).astype(BF16), one(high[e : e + 1] == place).astype(BF16)
        )
    named = one(named > 0.0).astype(BF16)
    marks_out[...] = jnp.zeros_like(marks_out)

    def mark(r, _):
        ids = row_of(rec_ref, r * 5)
        place = iota((128, rows), 0)
        found = dot(named, one(ids // 128 == place).astype(BF16))
        line = jnp.sum(jnp.where(ids % 128 == place, found, 0.0), axis=0, keepdims=True)
        for k in range(5):
            marks_out[r, pl.ds(k, 1), :] = line[:, k * 128 : (k + 1) * 128]
        return 0

    lax.fori_loop(0, groups, mark, 0)
    marks = marks_out[...].reshape(128, 128)
    ranks, before = ranks_of(marks)
    own_rank[...] = jnp.where(ranks < CAP, ranks, -1.0)
    sub = iota((128, 128), 0) % 8
    over = jnp.max(jnp.where((sub == 5) & (before > CAP), 1.0, 0.0), axis=0, keepdims=True)
    marks_out[...] = jnp.where(sub == 5, over, marks).reshape(groups, 8, 128)
    marks_in[pl.ds(c, 1)] = marks_out[pl.ds(c, 1)]

    pl.semaphore_wait(barrier, groups + team - 2)

    def mark_copy(k):
        p = chan_peer(k)
        return pltpu.make_async_remote_copy(
            marks_out.at[p], marks_in.at[c], mark_send.at[k], mark_recv.at[k],
            device_id=(t, p), device_id_type=MESH,
        )

    def start_mark(k, _):
        mark_copy(k).start()
        return 0

    lax.fori_loop(1, groups, start_mark, 0)

    shifted = jnp.broadcast_to(
        jnp.concatenate([taps_ref[...].astype(F32), jnp.zeros((1, 128), F32)], axis=1), (128, 256)
    )
    line = iota((128, 256), 0)
    for bit in range(7):
        shifted = jnp.where((line // (1 << bit)) % 2 == 1, pltpu.roll(shifted, 1 << bit, 1), shifted)
    block = shifted.astype(BF16)
    for k in range(length // 128):
        fold[pl.ds(k * 128, 128), :] = dot(block, table_ref[pl.ds(k * 128, 256), :]).astype(BF16)

    bins = iota((1, NB), 1)
    inv_count = 1.0 / (
        jnp.minimum(bins + SMOOTH, NB - 1) - jnp.maximum(bins - SMOOTH, 0) + 1
    ).astype(F32)

    def whiten(w):
        pltpu.make_async_copy(raw_ref.at[w], raw.at[w], load_sem.at[w]).wait()
        for half in range(2):
            here = pl.ds(half * (rows // 2), rows // 2)
            spectrum = dot(raw[w, here, :], fold[...])
            re, im = spectrum[:, :NB], spectrum[:, NB:]
            size = jnp.sqrt(re * re + im * im)
            big = size.astype(BF16)
            rest = (size - big.astype(F32)).astype(BF16)
            sums = dot(jnp.concatenate([big, rest], axis=1), band_ref[...])
            scale = 1.0 / (sums[:, :NB] * inv_count + sums[:, NB:] * (0.1 / NB) + 1e-06)
            white[w, here, :] = jnp.concatenate([re * scale, im * scale], axis=1).astype(BF16)

    def row_copy(w, k):
        p = chan_peer(k)
        return pltpu.make_async_remote_copy(
            send.at[w, p], recv.at[w, c], row_send.at[w, k], row_recv.at[w, k],
            device_id=(t, p), device_id_type=MESH,
        )

    def ship(w):
        send[w] = dot(pick[...], white[w]).astype(BF16).reshape(groups, CAP, 2 * NB)

        def start_row(k, _):
            row_copy(w, k).start()
            return 0

        lax.fori_loop(1, groups, start_row, 0)
        recv[w, pl.ds(c, 1)] = send[w, pl.ds(c, 1)]

    whiten(0)

    def end_mark(k, _):
        mark_copy(k).wait()
        return 0

    lax.fori_loop(1, groups, end_mark, 0)
    asked = marks_in[...].reshape(128, 128)
    flag_ref[...] = jnp.broadcast_to(
        jnp.max(jnp.where(sub == 5, asked, 0.0), axis=0, keepdims=True), (8, 128)
    )
    rank[...] = ranks_of(asked)[0]

    def choose(p, _):
        pick[pl.ds(pl.multiple_of(p * CAP, CAP), CAP), :] = one(
            row_of(rank, p * 8) == iota((CAP, rows), 0).astype(F32)
        ).astype(BF16)
        return 0

    lax.fori_loop(0, groups, choose, 0)
    ship(0)
    for w in range(1, windows):
        whiten(w)
        ship(w)

    def name_slots(j, _):
        found = jnp.zeros((8, 128), F32)
        for h in range(2):
            r = j * 2 + h
            ids = row_of(rec_ref, r * 5)
            ranked = row_of(own_rank, r * 8)
            spot = jnp.where(ranked >= 0.0, ranked + h * CAP, -1.0)
            chosen = one(spot == iota((128, rows), 0).astype(F32)).astype(BF16)
            kind = iota((8, rows), 0)
            values = jnp.where(
                kind == 0, (ids // 128).astype(F32), jnp.where(kind == 1, (ids % 128).astype(F32), 1.0)
            )
            found += dot_nt(values.astype(BF16), chosen)
        slot[pl.ds(j, 1), :] = jnp.where(
            found[2:3] > 0.0, found[0:1] * 128.0 + found[1:2], -1.0
        )
        return 0

    lax.fori_loop(0, groups // 2, name_slots, 0)
    columns = jnp.concatenate([ends.astype(F32), jnp.zeros((6, pair_count), F32)], axis=0).T
    for e in range(2):
        for j in range(groups // 2):
            take[e, :, j * 128 : (j + 1) * 128] = one(
                columns[:, e : e + 1] == slot[j : j + 1, :]
            ).astype(BF16)

    for w in range(windows):

        def end_row(k, _):
            row_copy(w, k).wait()
            return 0

        lax.fori_loop(1, groups, end_row, 0)
        arrived = recv[w].reshape(groups * CAP, 2 * NB)
        a = dot(take[0], arrived)
        b = dot(take[1], arrived)
        are, aim, bre, bim = a[:, :NB], a[:, NB:], b[:, :NB], b[:, NB:]
        product = jnp.concatenate([are * bre + aim * bim, aim * bre - are * bim], axis=1)
        if w == 0:
            acc[...] = product
        elif w < windows - 1:
            acc[...] += product
        else:
            part[...] = (
                ((acc[...] + product) * (1.0 / (windows * team))).astype(BF16).reshape(team, share, 2 * NB)
            )

    def part_copy(k):
        return pltpu.make_async_remote_copy(
            part.at[(t + k) % team], parts.at[t], part_send.at[k], part_recv.at[k],
            device_id=((t + k) % team, c), device_id_type=MESH,
        )

    def whole_copy(k):
        return pltpu.make_async_remote_copy(
            whole.at[t], whole.at[t], whole_send.at[k], whole_recv.at[k],
            device_id=((t + k) % team, c), device_id_type=MESH,
        )

    def start_part(k, _):
        part_copy(k).start()
        return 0

    def end_part(k, _):
        part_copy(k).wait()
        return 0

    def start_whole(k, _):
        whole_copy(k).start()
        return 0

    def end_whole(k, _):
        whole_copy(k).wait()
        return 0

    lax.fori_loop(1, team, start_part, 0)
    parts[pl.ds(t, 1)] = part[pl.ds(t, 1)]
    lax.fori_loop(1, team, end_part, 0)
    whole[pl.ds(t, 1)] = jnp.sum(parts[...].astype(F32), axis=0, keepdims=True).astype(BF16)
    lax.fori_loop(1, team, start_whole, 0)
    lax.fori_loop(1, team, end_whole, 0)
    out_ref[...] = whole[...].reshape(pair_count, 2 * NB).astype(F32)


def general(raw_blocks, fir_taps, recorder_channel, pairs, table, band):
    windows, rows, length = raw_blocks.shape
    offset = jnp.arange(length)[None, :] - jnp.arange(length)[:, None]
    filters = jnp.where(
        (offset >= 0) & (offset < fir_taps.shape[0]),
        jnp.take(fir_taps, jnp.clip(offset, 0, fir_taps.shape[0] - 1)),
        0,
    ).astype(BF16)
    rows_of = jnp.argsort(recorder_channel, stable=True)
    left, right = jnp.take(rows_of, pairs[:, 0]), jnp.take(rows_of, pairs[:, 1])
    smoother = band[:NB, :NB].astype(F32)
    smoother = smoother / jnp.sum(smoother, axis=0, keepdims=True)

    def one_window(total, window):
        filtered = dot(window, filters).astype(BF16)
        spectrum = dot(filtered, table[:length])
        re, im = spectrum[:, :NB], spectrum[:, NB:]
        size = jnp.sqrt(re * re + im * im)
        smoothed = jnp.dot(size, smoother, precision=lax.Precision.HIGHEST)
        scale = 1.0 / (smoothed + 0.1 * jnp.mean(size, axis=-1, keepdims=True) + 1e-06)
        whitened = jnp.concatenate([re * scale, im * scale], axis=1).astype(BF16)
        everything = lax.all_gather(whitened, "chan", axis=0, tiled=True)
        a = jnp.take(everything, left, axis=0).astype(F32)
        b = jnp.take(everything, right, axis=0).astype(F32)
        are, aim, bre, bim = a[:, :NB], a[:, NB:], b[:, :NB], b[:, NB:]
        return total + jnp.concatenate([are * bre + aim * bim, aim * bre - are * bim], axis=1), None

    total, _ = lax.scan(one_window, jnp.zeros((pairs.shape[0], 2 * NB), F32), raw_blocks)
    return lax.psum(total, "tm") / (windows * lax.axis_size("tm"))


def local(raw_blocks, fir_taps, recorder_channel, pairs):
    windows, rows, length = raw_blocks.shape
    pair_count = pairs.shape[0]
    groups, team = 16, 8
    share = pair_count // team
    table = jnp.asarray(table_values(length, 128))
    band = jnp.asarray(band_values())
    vmem = pl.BlockSpec(memory_space=pltpu.VMEM)
    dma = pltpu.SemaphoreType.DMA
    out, flag = pl.pallas_call(
        kernel,
        out_shape=[
            jax.ShapeDtypeStruct((pair_count, 2 * NB), F32),
            jax.ShapeDtypeStruct((8, 128), F32),
        ],
        in_specs=[pl.BlockSpec(memory_space=pl.ANY)] + [vmem] * 5,
        out_specs=[vmem, vmem],
        scratch_shapes=[
            pltpu.VMEM((windows, rows, length), BF16),
            pltpu.VMEM((length, 2 * NB), BF16),
            pltpu.VMEM((windows, rows, 2 * NB), BF16),
            pltpu.VMEM((groups, 8, 128), F32),
            pltpu.VMEM((groups, 8, 128), F32),
            pltpu.VMEM((groups * 8, 128), F32),
            pltpu.VMEM((groups * 8, 128), F32),
            pltpu.VMEM((groups * CAP, rows), BF16),
            pltpu.VMEM((windows, groups, CAP, 2 * NB), BF16),
            pltpu.VMEM((windows, groups, CAP, 2 * NB), BF16),
            pltpu.VMEM((groups // 2, 128), F32),
            pltpu.VMEM((2, pair_count, groups * CAP), BF16),
            pltpu.VMEM((pair_count, 2 * NB), F32),
            pltpu.VMEM((team, share, 2 * NB), BF16),
            pltpu.VMEM((team, share, 2 * NB), BF16),
            pltpu.VMEM((team, share, 2 * NB), BF16),
            dma((windows,)),
            dma((groups,)),
            dma((groups,)),
            dma((windows, groups)),
            dma((windows, groups)),
            dma((team,)),
            dma((team,)),
            dma((team,)),
            dma((team,)),
        ],
        compiler_params=pltpu.CompilerParams(
            collective_id=0, has_side_effects=True, vmem_limit_bytes=48 * 2**20
        ),
    )(raw_blocks, fir_taps.reshape(1, -1), recorder_channel.reshape(-1, 128), pairs.T, table, band)
    return lax.cond(
        flag[0, 0] > 0.0,
        lambda: general(raw_blocks, fir_taps, recorder_channel, pairs, table, band),
        lambda: out,
    )


def solution(mesh):
    in_specs = (P("tm", "chan", None), P(), P(), P("chan", None))
    out_specs = P("chan", None)
    return jax.shard_map(local, mesh=mesh, in_specs=in_specs, out_specs=out_specs, check_vma=False)
```

```python
import jax
import jax.numpy as jnp
import numpy as np
from jax import lax
from jax.experimental import pallas as pl
from jax.experimental.pallas import tpu as pltpu
from jax.sharding import PartitionSpec as P

NB = 128
SMOOTH = 4
CAP = 56
SLOT = 64
MESH = pl.DeviceIdType.MESH
F32 = jnp.float32
BF16 = jnp.bfloat16
NT = (((1,), (1,)), ((), ()))


def table_values(length, extra):
    samples = np.arange(length, dtype=np.int64)
    freqs = np.arange(1, NB + 1, dtype=np.int64)
    angles = (samples[:, None] * freqs[None, :] % length).astype(np.float32) * np.float32(2.0 * np.pi / length)
    table = np.concatenate([np.cos(angles), -np.sin(angles)], axis=1)
    return np.concatenate([table, np.zeros((extra, 2 * NB), np.float32)]).astype(BF16)


def iota(shape, dim):
    return lax.broadcasted_iota(jnp.int32, shape, dim)


def dot(left, right):
    return jnp.dot(left, right, preferred_element_type=F32)


def dot_nt(left, right):
    return lax.dot_general(left, right, NT, preferred_element_type=F32)


def one(condition):
    return jnp.where(condition, 1.0, 0.0)


def ranks_of(marks):
    row, col = iota((128, 128), 0), iota((128, 128), 1)
    marks = jnp.where(row % 8 < 5, marks, 0.0)
    held = marks.astype(BF16)
    upto = dot(held, one(row <= col).astype(BF16))
    totals = dot(held, jnp.ones((128, 128), BF16))
    before = dot(one((row // 8 == col // 8) & (col < row)).astype(BF16), totals.astype(BF16))
    return jnp.where(marks > 0.0, upto + before - 1.0, -1.0), before


def row_of(ref, first):
    return jnp.concatenate([ref[pl.ds(first + k, 1), :] for k in range(5)], axis=1)


def roll_half(value):
    return pltpu.roll(value, NB // 2, 1)


def kernel(
    raw_hbm, taps_hbm, rec_hbm, pairs_hbm, table_hbm, out_ref, flag_ref,
    raw, taps, rec, pairs, table, fold, white, marks_out, marks_in, rank, own_rank, send, recv, arrived, slot, take,
    part, parts, whole,
    load_sem, small_sem, mark_send, mark_recv, row_send, row_recv, part_send, part_recv, whole_send, whole_recv,
):
    t, c = lax.axis_index("tm"), lax.axis_index("chan")
    y, z = c // 4, c % 4
    windows, rows, length = raw.shape
    groups = 16
    team = 8
    pair_count = out_ref.shape[0]
    share = pair_count // team

    small = [(pairs_hbm, pairs), (rec_hbm, rec), (taps_hbm, taps), (table_hbm, table)]

    def small_copy(i):
        return pltpu.make_async_copy(small[i][0], small[i][1], small_sem.at[i])

    def load_copy(w):
        return pltpu.make_async_copy(raw_hbm.at[w], raw.at[w], load_sem.at[w])

    for i in range(len(small)):
        small_copy(i).start()
    for w in range(windows):
        load_copy(w).start()

    def chan_peer(k):
        return (y + k // 4) % 4 * 4 + (z + k % 4) % 4

    def chan_from(k):
        return (y + 4 - k // 4) % 4 * 4 + (z + 4 - k % 4) % 4

    barrier = pltpu.get_barrier_semaphore()

    def greet_chan(k, _):
        pl.semaphore_signal(barrier, inc=1, device_id=(t, chan_peer(k)), device_id_type=MESH)
        return 0

    def greet_tm(k, _):
        pl.semaphore_signal(barrier, inc=1, device_id=((t + k) % team, c), device_id_type=MESH)
        return 0

    lax.fori_loop(1, groups, greet_chan, 0)
    lax.fori_loop(1, team, greet_tm, 0)

    small_copy(0).wait()
    ends = pairs[...]
    high, low = ends // 128, ends % 128
    place = iota((128, pair_count), 0)
    named = jnp.zeros((128, 128), F32)
    for e in range(2):
        named += dot_nt(
            one(low[e : e + 1] == place).astype(BF16), one(high[e : e + 1] == place).astype(BF16)
        )
    named = one(named > 0.0).astype(BF16)
    marks_out[...] = jnp.zeros_like(marks_out)
    small_copy(1).wait()

    def mark(j, _):
        ids = jnp.concatenate([rec[pl.ds(j * 10 + k, 1), :] for k in range(10)], axis=1)
        place = iota((128, 2 * rows), 0)
        found = dot(named, one(ids // 128 == place).astype(BF16))
        line = jnp.sum(jnp.where(ids % 128 == place, found, 0.0), axis=0, keepdims=True)
        for k in range(10):
            marks_out[j * 2 + k // 5, pl.ds(k % 5, 1), :] = line[:, k * 128 : (k + 1) * 128]
        return 0

    lax.fori_loop(0, groups // 2, mark, 0)
    marks = marks_out[...].reshape(128, 128)
    ranks, before = ranks_of(marks)
    own_rank[...] = jnp.where(ranks < CAP, ranks, -1.0)
    sub = iota((128, 128), 0) % 8
    over = jnp.max(jnp.where((sub == 5) & (before > CAP), 1.0, 0.0), axis=0, keepdims=True)
    marks_out[...] = jnp.where(sub == 5, over, marks).reshape(groups, 8, 128)
    marks_in[pl.ds(c, 1)] = marks_out[pl.ds(c, 1)]

    pl.semaphore_wait(barrier, groups + team - 2)

    def mark_copy(k):
        p = chan_peer(k)
        return pltpu.make_async_remote_copy(
            marks_out.at[p], marks_in.at[c], mark_send.at[k], mark_recv.at[k],
            device_id=(t, p), device_id_type=MESH,
        )

    def start_mark(k, _):
        mark_copy(k).start()
        return 0

    lax.fori_loop(1, groups, start_mark, 0)

    small_copy(2).wait()
    shifted = jnp.broadcast_to(
        jnp.concatenate([taps[...].astype(F32), jnp.zeros((1, 128), F32)], axis=1), (128, 256)
    )
    line = iota((128, 256), 0)
    for bit in range(7):
        shifted = jnp.where((line // (1 << bit)) % 2 == 1, pltpu.roll(shifted, 1 << bit, 1), shifted)
    block = shifted.astype(BF16)
    small_copy(3).wait()
    for k in range(length // 128):
        fold[pl.ds(k * 128, 128), :] = dot(block, table[pl.ds(k * 128, 256), :]).astype(BF16)

    bins = iota((1, NB), 1)
    inv_count = 1.0 / (
        jnp.minimum(bins + SMOOTH, NB - 1) - jnp.maximum(bins - SMOOTH, 0) + 1
    ).astype(F32)
    from_bin, to_bin = iota((2 * NB, 2 * NB), 0) % NB, iota((2 * NB, 2 * NB), 1)
    near = (from_bin - to_bin <= SMOOTH) & (to_bin - from_bin <= SMOOTH)
    band = one(near | (to_bin >= NB)).astype(BF16)
    lower = iota((rows // 2, NB), 1) < NB // 2

    for w in range(windows):
        load_copy(w).wait()
        for half in range(2):
            here = pl.ds(half * (rows // 2), rows // 2)
            spectrum = dot(raw[w, here, :], fold[...])
            re, im = spectrum[:, :NB], spectrum[:, NB:]
            size = jnp.sqrt(re * re + im * im)
            big = size.astype(BF16)
            rest = (size - big.astype(F32)).astype(BF16)
            sums = dot(jnp.concatenate([big, rest], axis=1), band)
            scale = 1.0 / (sums[:, :NB] * inv_count + sums[:, NB:] * (0.1 / NB) + 1e-06)
            re, im = re * scale, im * scale
            lanes = pl.ds(w * NB, NB)
            white[0, here, lanes] = jnp.where(lower, re, roll_half(im)).astype(BF16)
            white[1, here, lanes] = jnp.where(lower, roll_half(re), im).astype(BF16)

    def end_mark(k, _):
        mark_copy(k).wait_recv()
        return 0

    lax.fori_loop(1, groups, end_mark, 0)
    asked = marks_in[...].reshape(128, 128)
    flag_ref[...] = jnp.broadcast_to(
        jnp.max(jnp.where(sub == 5, asked, 0.0), axis=0, keepdims=True), (8, 128)
    )
    rank[...] = ranks_of(asked)[0]

    def row_copy(h, k):
        p = chan_peer(k)
        return pltpu.make_async_remote_copy(
            send.at[h, p], recv.at[h, c], row_send.at[h, k], row_recv.at[h, k],
            device_id=(t, p), device_id_type=MESH,
        )

    def ship(h):
        for k in (8, 4, 12, 0):
            picks = []
            for m in range(4):
                ranked = row_of(rank, chan_peer(k + m) * 8)
                picks.append(one(ranked == iota((CAP, rows), 0).astype(F32)))
            chosen = dot(jnp.concatenate(picks, axis=0).astype(BF16), white[h])
            for m in range(4):
                mine = chosen[m * CAP : (m + 1) * CAP]
                send[h, pl.ds(chan_peer(k + m), 1)] = jnp.concatenate(
                    [mine[:, : 2 * NB], mine[:, 2 * NB :]], axis=0
                ).astype(BF16)[None]
            for m in (2, 1, 3, 0):
                if k + m:
                    row_copy(h, k + m).start()

    ship(0)
    ship(1)

    def name_slots(j, _):
        found = jnp.zeros((8, 128), F32)
        for h in range(2):
            r = j * 2 + h
            ids = row_of(rec, r * 5)
            ranked = row_of(own_rank, r * 8)
            spot = jnp.where(ranked >= 0.0, ranked + h * SLOT, -1.0)
            chosen = one(spot == iota((128, rows), 0).astype(F32)).astype(BF16)
            kind = iota((8, rows), 0)
            values = jnp.where(
                kind == 0, (ids // 128).astype(F32), jnp.where(kind == 1, (ids % 128).astype(F32), 1.0)
            )
            found += dot_nt(values.astype(BF16), chosen)
        slot[pl.ds(j, 1), :] = jnp.where(
            found[2:3] > 0.0, found[0:1] * 128.0 + found[1:2], -1.0
        )
        return 0

    lax.fori_loop(0, groups // 2, name_slots, 0)
    columns = jnp.concatenate([ends.astype(F32), jnp.zeros((6, pair_count), F32)], axis=0).T
    for e in range(2):
        for j in range(groups // 2):
            take[e, :, j * 128 : (j + 1) * 128] = one(
                columns[:, e : e + 1] == slot[j : j + 1, :]
            ).astype(BF16)

    def part_copy(h, k):
        return pltpu.make_async_remote_copy(
            part.at[h, (t + k) % team], parts.at[h, t], part_send.at[h, k], part_recv.at[h, k],
            device_id=((t + k) % team, c), device_id_type=MESH,
        )

    def whole_copy(h, k):
        return pltpu.make_async_remote_copy(
            whole.at[h, t], whole.at[h, t], whole_send.at[h, k], whole_recv.at[h, k],
            device_id=((t + k) % team, c), device_id_type=MESH,
        )

    def settle(h, r):
        got = recv[h, pl.ds(r, 1)][0].astype(F32)
        arrived[pl.ds(pl.multiple_of(r * SLOT, SLOT), SLOT), :] = jnp.concatenate(
            [
                jnp.concatenate([got[:CAP], got[CAP:]], axis=1),
                jnp.zeros((SLOT - CAP, 4 * NB), F32),
            ],
            axis=0,
        ).astype(BF16)

    for h in range(2):
        recv[h, pl.ds(c, 1)] = send[h, pl.ds(c, 1)]
        settle(h, c)

        def end_row(k, _, h=h):
            row_copy(h, k).wait_recv()
            settle(h, chan_from(k))
            return 0

        lax.fori_loop(1, groups, end_row, 0)
        for q in range(2):
            some = pl.ds(q * (pair_count // 2), pair_count // 2)
            a = dot(take[0, some, :], arrived[...])
            b = dot(take[1, some, :], arrived[...])
            straight = jnp.zeros((pair_count // 2, NB), F32)
            crossed = jnp.zeros((pair_count // 2, NB), F32)
            for w in range(windows):
                aw, bw = a[:, w * NB : (w + 1) * NB], b[:, w * NB : (w + 1) * NB]
                straight += aw * bw
                crossed += aw * roll_half(bw)
            lower = iota((pair_count // 2, NB), 1) < NB // 2
            product = jnp.where(lower, straight + roll_half(straight), crossed - roll_half(crossed))
            part[h, pl.ds(q * (team // 2), team // 2)] = (
                (product * (1.0 / (windows * team))).astype(BF16).reshape(team // 2, share, NB)
            )

        def start_part(k, _, h=h):
            part_copy(h, k).start()
            return 0

        def end_part(k, _, h=h):
            part_copy(h, k).wait_recv()
            return 0

        def start_whole(k, _, h=h):
            whole_copy(h, k).start()
            return 0

        lax.fori_loop(1, team, start_part, 0)
        parts[h, pl.ds(t, 1)] = part[h, pl.ds(t, 1)]
        lax.fori_loop(1, team, end_part, 0)
        whole[h, pl.ds(t, 1)] = jnp.sum(parts[h].astype(F32), axis=0, keepdims=True).astype(BF16)
        lax.fori_loop(1, team, start_whole, 0)

    def end_whole(k, _):
        for h in range(2):
            whole_copy(h, k).wait_recv()
        return 0

    lax.fori_loop(1, team, end_whole, 0)
    first = whole[0].astype(F32).reshape(pair_count, NB)
    second = whole[1].astype(F32).reshape(pair_count, NB)
    lower = iota((pair_count, NB), 1) < NB // 2
    out_ref[:, :NB] = jnp.where(lower, first, roll_half(second))
    out_ref[:, NB:] = jnp.where(lower, roll_half(first), second)

    def end_sends(k, _):
        mark_copy(k).wait_send()
        for h in range(2):
            row_copy(h, k).wait_send()
        return 0

    def end_team_sends(k, _):
        for h in range(2):
            part_copy(h, k).wait_send()
            whole_copy(h, k).wait_send()
        return 0

    lax.fori_loop(1, groups, end_sends, 0)
    lax.fori_loop(1, team, end_team_sends, 0)


def spread(block, axis):
    count = lax.axis_size(axis)
    return lax.all_to_all(jnp.broadcast_to(block[None], (count,) + block.shape), axis, 0, 0)


def general(raw_blocks, fir_taps, recorder_channel, pairs, table):
    windows, rows, length = raw_blocks.shape
    offset = jnp.arange(length)[None, :] - jnp.arange(length)[:, None]
    filters = jnp.where(
        (offset >= 0) & (offset < fir_taps.shape[0]),
        jnp.take(fir_taps, jnp.clip(offset, 0, fir_taps.shape[0] - 1)),
        0,
    ).astype(BF16)
    channels = recorder_channel.shape[0]
    rows_of = jnp.zeros((channels,), jnp.int32).at[recorder_channel].set(jnp.arange(channels, dtype=jnp.int32))
    left, right = jnp.take(rows_of, pairs[:, 0]), jnp.take(rows_of, pairs[:, 1])
    bins = jnp.arange(NB)
    near = (jnp.abs(bins[:, None] - bins[None, :]) <= SMOOTH).astype(F32)
    smoother = near / jnp.sum(near, axis=0, keepdims=True)

    def one_window(total, window):
        filtered = dot(window, filters).astype(BF16)
        spectrum = dot(filtered, table[:length])
        re, im = spectrum[:, :NB], spectrum[:, NB:]
        size = jnp.sqrt(re * re + im * im)
        smoothed = jnp.dot(size, smoother, precision=lax.Precision.HIGHEST)
        scale = 1.0 / (smoothed + 0.1 * jnp.mean(size, axis=-1, keepdims=True) + 1e-06)
        whitened = jnp.concatenate([re * scale, im * scale], axis=1).astype(BF16)
        everything = spread(whitened, "chan").reshape(channels, 2 * NB)
        a = jnp.take(everything, left, axis=0).astype(F32)
        b = jnp.take(everything, right, axis=0).astype(F32)
        are, aim, bre, bim = a[:, :NB], a[:, NB:], b[:, :NB], b[:, NB:]
        return total + jnp.concatenate([are * bre + aim * bim, aim * bre - are * bim], axis=1), None

    total, _ = lax.scan(one_window, jnp.zeros((pairs.shape[0], 2 * NB), F32), raw_blocks)
    return jnp.sum(spread(total, "tm"), axis=0) / (windows * lax.axis_size("tm"))


def local(raw_blocks, fir_taps, recorder_channel, pairs):
    windows, rows, length = raw_blocks.shape
    pair_count = pairs.shape[0]
    groups, team = 16, 8
    share = pair_count // team
    table = jnp.asarray(table_values(length, 128))
    hbm = pl.BlockSpec(memory_space=pltpu.HBM)
    vmem = pl.BlockSpec(memory_space=pltpu.VMEM)
    dma = pltpu.SemaphoreType.DMA
    out, flag = pl.pallas_call(
        kernel,
        out_shape=[
            jax.ShapeDtypeStruct((pair_count, 2 * NB), F32),
            jax.ShapeDtypeStruct((8, 128), F32),
        ],
        in_specs=[hbm] * 5,
        out_specs=[vmem, vmem],
        scratch_shapes=[
            pltpu.VMEM((windows, rows, length), BF16),
            pltpu.VMEM((1, 128), BF16),
            pltpu.VMEM((80, 128), jnp.int32),
            pltpu.VMEM((2, pair_count), jnp.int32),
            pltpu.VMEM((length + 128, 2 * NB), BF16),
            pltpu.VMEM((length, 2 * NB), BF16),
            pltpu.VMEM((2, rows, windows * NB), BF16),
            pltpu.VMEM((groups, 8, 128), F32),
            pltpu.VMEM((groups, 8, 128), F32),
            pltpu.VMEM((groups * 8, 128), F32),
            pltpu.VMEM((groups * 8, 128), F32),
            pltpu.VMEM((2, groups, 2 * CAP, 2 * NB), BF16),
            pltpu.VMEM((2, groups, 2 * CAP, 2 * NB), BF16),
            pltpu.VMEM((groups * SLOT, windows * NB), BF16),
            pltpu.VMEM((groups // 2, 128), F32),
            pltpu.VMEM((2, pair_count, groups * SLOT), BF16),
            pltpu.VMEM((2, team, share, NB), BF16),
            pltpu.VMEM((2, team, share, NB), BF16),
            pltpu.VMEM((2, team, share, NB), BF16),
            dma((windows,)),
            dma((4,)),
            dma((groups,)),
            dma((groups,)),
            dma((2, groups)),
            dma((2, groups)),
            dma((2, team)),
            dma((2, team)),
            dma((2, team)),
            dma((2, team)),
        ],
        compiler_params=pltpu.CompilerParams(
            collective_id=0, has_side_effects=True, vmem_limit_bytes=40 * 2**20
        ),
    )(raw_blocks, fir_taps.reshape(1, -1), recorder_channel.reshape(-1, 128), pairs.T, table)
    return lax.cond(
        flag[0, 0] > 0.0,
        lambda: general(raw_blocks, fir_taps, recorder_channel, pairs, table),
        lambda: out,
    )


def solution(mesh):
    in_specs = (P("tm", "chan", None), P(), P(), P("chan", None))
    out_specs = P("chan", None)
    return jax.shard_map(local, mesh=mesh, in_specs=in_specs, out_specs=out_specs, check_vma=False)
```

```python
import jax
import jax.numpy as jnp
import numpy as np
from jax import lax
from jax.experimental import pallas as pl
from jax.experimental.pallas import tpu as pltpu
from jax.sharding import PartitionSpec as P

NB = 128
SMOOTH = 4
CAP = 56
SLOT = 64
MESH = pl.DeviceIdType.MESH
F32 = jnp.float32
BF16 = jnp.bfloat16
NT = (((1,), (1,)), ((), ()))


def table_values(length, extra):
    samples = np.arange(length, dtype=np.int64)
    freqs = np.arange(1, NB + 1, dtype=np.int64)
    angles = (samples[:, None] * freqs[None, :] % length).astype(np.float32) * np.float32(2.0 * np.pi / length)
    table = np.concatenate([np.cos(angles), -np.sin(angles)], axis=1)
    return np.concatenate([table, np.zeros((extra, 2 * NB), np.float32)]).astype(BF16)


def iota(shape, dim):
    return lax.broadcasted_iota(jnp.int32, shape, dim)


def dot(left, right):
    return jnp.dot(left, right, preferred_element_type=F32)


def dot_nt(left, right):
    return lax.dot_general(left, right, NT, preferred_element_type=F32)


def one(condition):
    return jnp.where(condition, 1.0, 0.0)


def ranks_of(marks):
    row, col = iota((128, 128), 0), iota((128, 128), 1)
    marks = jnp.where(row % 8 < 5, marks, 0.0)
    held = marks.astype(BF16)
    upto = dot(held, one(row <= col).astype(BF16))
    totals = dot(held, jnp.ones((128, 128), BF16))
    before = dot(one((row // 8 == col // 8) & (col < row)).astype(BF16), totals.astype(BF16))
    return jnp.where(marks > 0.0, upto + before - 1.0, -1.0), before


def row_of(ref, first):
    return jnp.concatenate([ref[pl.ds(first + k, 1), :] for k in range(5)], axis=1)


def roll_half(value):
    return pltpu.roll(value, NB // 2, 1)


def kernel(
    raw_hbm, taps_hbm, rec_hbm, pairs_hbm, table_hbm, out_ref, flag_ref,
    raw, taps, rec, pairs, table, fold, white, marks_out, marks_in, rank, own_rank, send, recv, arrived, slot, take,
    part, parts, whole,
    load_sem, small_sem, mark_send, mark_recv, row_send, row_recv, part_send, part_recv, whole_send, whole_recv,
):
    t, c = lax.axis_index("tm"), lax.axis_index("chan")
    y, z = c // 4, c % 4
    windows, rows, length = raw.shape
    groups = 16
    team = 8
    pair_count = out_ref.shape[0]
    share = pair_count // team

    small = [(pairs_hbm, pairs), (rec_hbm, rec), (taps_hbm, taps), (table_hbm, table)]

    def small_copy(i):
        return pltpu.make_async_copy(small[i][0], small[i][1], small_sem.at[i])

    def load_copy(w):
        return pltpu.make_async_copy(raw_hbm.at[w], raw.at[w], load_sem.at[w])

    for i in range(len(small)):
        small_copy(i).start()
    for w in range(windows):
        load_copy(w).start()

    def chan_peer(k):
        return (y + k // 4) % 4 * 4 + (z + k % 4) % 4

    def chan_from(k):
        return (y + 4 - k // 4) % 4 * 4 + (z + 4 - k % 4) % 4

    barrier = pltpu.get_barrier_semaphore()

    def greet_chan(k, _):
        pl.semaphore_signal(barrier, inc=1, device_id=(t, chan_peer(k)), device_id_type=MESH)
        return 0

    def greet_tm(k, _):
        pl.semaphore_signal(barrier, inc=1, device_id=((t + k) % team, c), device_id_type=MESH)
        return 0

    lax.fori_loop(1, groups, greet_chan, 0)
    lax.fori_loop(1, team, greet_tm, 0)

    small_copy(0).wait()
    ends = pairs[...]
    high, low = ends // 128, ends % 128
    place = iota((128, pair_count), 0)
    named = jnp.zeros((128, 128), F32)
    for e in range(2):
        named += dot_nt(
            one(low[e : e + 1] == place).astype(BF16), one(high[e : e + 1] == place).astype(BF16)
        )
    named = one(named > 0.0).astype(BF16)
    marks_out[...] = jnp.zeros_like(marks_out)
    small_copy(1).wait()

    def mark(j, _):
        ids = jnp.concatenate([rec[pl.ds(j * 10 + k, 1), :] for k in range(10)], axis=1)
        place = iota((128, 2 * rows), 0)
        found = dot(named, one(ids // 128 == place).astype(BF16))
        line = jnp.sum(jnp.where(ids % 128 == place, found, 0.0), axis=0, keepdims=True)
        for k in range(10):
            marks_out[j * 2 + k // 5, pl.ds(k % 5, 1), :] = line[:, k * 128 : (k + 1) * 128]
        return 0

    lax.fori_loop(0, groups // 2, mark, 0)
    marks = marks_out[...].reshape(128, 128)
    ranks, before = ranks_of(marks)
    own_rank[...] = jnp.where(ranks < CAP, ranks, -1.0)
    sub = iota((128, 128), 0) % 8
    over = jnp.max(jnp.where((sub == 5) & (before > CAP), 1.0, 0.0), axis=0, keepdims=True)
    marks_out[...] = jnp.where(sub == 5, over, marks).reshape(groups, 8, 128)
    marks_in[pl.ds(c, 1)] = marks_out[pl.ds(c, 1)]

    pl.semaphore_wait(barrier, groups + team - 2)

    def mark_copy(k):
        p = chan_peer(k)
        return pltpu.make_async_remote_copy(
            marks_out.at[p], marks_in.at[c], mark_send.at[k], mark_recv.at[k],
            device_id=(t, p), device_id_type=MESH,
        )

    def start_mark(k, _):
        mark_copy(k).start()
        return 0

    lax.fori_loop(1, groups, start_mark, 0)

    small_copy(2).wait()
    shifted = jnp.broadcast_to(
        jnp.concatenate([taps[...].astype(F32), jnp.zeros((1, 128), F32)], axis=1), (128, 256)
    )
    line = iota((128, 256), 0)
    for bit in range(7):
        shifted = jnp.where((line // (1 << bit)) % 2 == 1, pltpu.roll(shifted, 1 << bit, 1), shifted)
    block = shifted.astype(BF16)
    small_copy(3).wait()
    for k in range(length // 128):
        fold[pl.ds(k * 128, 128), :] = dot(block, table[pl.ds(k * 128, 256), :]).astype(BF16)

    bins = iota((1, NB), 1)
    inv_count = 1.0 / (
        jnp.minimum(bins + SMOOTH, NB - 1) - jnp.maximum(bins - SMOOTH, 0) + 1
    ).astype(F32)
    from_bin, to_bin = iota((2 * NB, 2 * NB), 0) % NB, iota((2 * NB, 2 * NB), 1)
    near = (from_bin - to_bin <= SMOOTH) & (to_bin - from_bin <= SMOOTH)
    band = one(near | (to_bin >= NB)).astype(BF16)
    lower = iota((rows // 2, NB), 1) < NB // 2

    for w in range(windows):
        load_copy(w).wait()
        for half in range(2):
            here = pl.ds(half * (rows // 2), rows // 2)
            spectrum = dot(raw[w, here, :], fold[...])
            re, im = spectrum[:, :NB], spectrum[:, NB:]
            size = jnp.sqrt(re * re + im * im)
            big = size.astype(BF16)
            rest = (size - big.astype(F32)).astype(BF16)
            sums = dot(jnp.concatenate([big, rest], axis=1), band)
            scale = 1.0 / (sums[:, :NB] * inv_count + sums[:, NB:] * (0.1 / NB) + 1e-06)
            re, im = re * scale, im * scale
            lanes = pl.ds(w * NB, NB)
            white[0, here, lanes] = jnp.where(lower, re, roll_half(im)).astype(BF16)
            white[1, here, lanes] = jnp.where(lower, roll_half(re), im).astype(BF16)

    def end_mark(k, _):
        mark_copy(k).wait_recv()
        return 0

    lax.fori_loop(1, groups, end_mark, 0)
    asked = marks_in[...].reshape(128, 128)
    flag_ref[0] = jnp.max(jnp.where(sub == 5, asked, 0.0))
    rank[...] = ranks_of(asked)[0]

    def row_copy(h, k):
        p = chan_peer(k)
        return pltpu.make_async_remote_copy(
            send.at[h, p], recv.at[h, c], row_send.at[h, k], row_recv.at[h, k],
            device_id=(t, p), device_id_type=MESH,
        )

    def ship(h):
        for k in (8, 4, 12, 0):
            picks = []
            for m in range(4):
                ranked = row_of(rank, chan_peer(k + m) * 8)
                picks.append(one(ranked == iota((CAP, rows), 0).astype(F32)))
            chosen = dot(jnp.concatenate(picks, axis=0).astype(BF16), white[h])
            for m in range(4):
                mine = chosen[m * CAP : (m + 1) * CAP]
                send[h, pl.ds(chan_peer(k + m), 1)] = jnp.concatenate(
                    [mine[:, : 2 * NB], mine[:, 2 * NB :]], axis=0
                ).astype(BF16)[None]
            for m in (2, 1, 3, 0):
                if k + m:
                    row_copy(h, k + m).start()

    ship(0)
    ship(1)

    def name_slots(j, _):
        found = jnp.zeros((8, 128), F32)
        for h in range(2):
            r = j * 2 + h
            ids = row_of(rec, r * 5)
            ranked = row_of(own_rank, r * 8)
            spot = jnp.where(ranked >= 0.0, ranked + h * SLOT, -1.0)
            chosen = one(spot == iota((128, rows), 0).astype(F32)).astype(BF16)
            kind = iota((8, rows), 0)
            values = jnp.where(
                kind == 0, (ids // 128).astype(F32), jnp.where(kind == 1, (ids % 128).astype(F32), 1.0)
            )
            found += dot_nt(values.astype(BF16), chosen)
        slot[pl.ds(j, 1), :] = jnp.where(
            found[2:3] > 0.0, found[0:1] * 128.0 + found[1:2], -1.0
        )
        return 0

    lax.fori_loop(0, groups // 2, name_slots, 0)
    columns = jnp.concatenate([ends.astype(F32), jnp.zeros((6, pair_count), F32)], axis=0).T
    for e in range(2):
        for j in range(groups // 2):
            take[e, :, j * 128 : (j + 1) * 128] = one(
                columns[:, e : e + 1] == slot[j : j + 1, :]
            ).astype(BF16)

    def part_copy(h, to, source):
        return pltpu.make_async_remote_copy(
            part.at[h, to], parts.at[h, source], part_send.at[h, to], part_recv.at[h, source],
            device_id=(to, c), device_id_type=MESH,
        )

    def whole_copy(h, k):
        return pltpu.make_async_remote_copy(
            whole.at[h, t], whole.at[h, t], whole_send.at[h, k], whole_recv.at[h, k],
            device_id=((t + k) % team, c), device_id_type=MESH,
        )

    def settle(h, r):
        got = recv[h, pl.ds(r, 1)][0].astype(F32)
        arrived[pl.ds(pl.multiple_of(r * SLOT, SLOT), SLOT), :] = jnp.concatenate(
            [
                jnp.concatenate([got[:CAP], got[CAP:]], axis=1),
                jnp.zeros((SLOT - CAP, 4 * NB), F32),
            ],
            axis=0,
        ).astype(BF16)

    def add_parts(h):
        def end_part(k, _):
            part_copy(h, 0, (t + k) % team).wait_recv()
            return 0

        def start_whole(k, _):
            whole_copy(h, k).start()
            return 0

        parts[h, pl.ds(t, 1)] = part[h, pl.ds(t, 1)]
        lax.fori_loop(1, team, end_part, 0)
        whole[h, pl.ds(t, 1)] = jnp.sum(parts[h].astype(F32), axis=0, keepdims=True).astype(BF16)
        lax.fori_loop(1, team, start_whole, 0)

    for h in range(2):
        recv[h, pl.ds(c, 1)] = send[h, pl.ds(c, 1)]
        settle(h, c)

        def end_row(k, _, h=h):
            row_copy(h, k).wait_recv()
            settle(h, chan_from(k))
            return 0

        lax.fori_loop(1, groups, end_row, 0)
        if h:
            add_parts(0)
        for q in range(2):
            some = pl.ds(q * (pair_count // 2), pair_count // 2)
            a = dot(take[0, some, :], arrived[...])
            b = dot(take[1, some, :], arrived[...])
            straight = jnp.zeros((pair_count // 2, NB), F32)
            crossed = jnp.zeros((pair_count // 2, NB), F32)
            for w in range(windows):
                aw, bw = a[:, w * NB : (w + 1) * NB], b[:, w * NB : (w + 1) * NB]
                straight += aw * bw
                crossed += aw * roll_half(bw)
            lower = iota((pair_count // 2, NB), 1) < NB // 2
            product = jnp.where(lower, straight + roll_half(straight), crossed - roll_half(crossed))
            part[h, pl.ds(q * (team // 2), team // 2)] = (
                (product * (1.0 / (windows * team))).astype(BF16).reshape(team // 2, share, NB)
            )

            def start_part(k, _, h=h):
                @pl.when(k != t)
                def _():
                    part_copy(h, k, t).start()

                return 0

            lax.fori_loop(q * (team // 2), (q + 1) * (team // 2), start_part, 0)
    add_parts(1)

    def end_whole(k, _):
        for h in range(2):
            whole_copy(h, k).wait_recv()
        return 0

    lax.fori_loop(1, team, end_whole, 0)
    first = whole[0].astype(F32).reshape(pair_count, NB)
    second = whole[1].astype(F32).reshape(pair_count, NB)
    lower = iota((pair_count, NB), 1) < NB // 2
    out_ref[:, :NB] = jnp.where(lower, first, roll_half(second)).astype(BF16)
    out_ref[:, NB:] = jnp.where(lower, roll_half(first), second).astype(BF16)

    def end_sends(k, _):
        mark_copy(k).wait_send()
        for h in range(2):
            row_copy(h, k).wait_send()
        return 0

    def end_team_sends(k, _):
        for h in range(2):
            part_copy(h, (t + k) % team, t).wait_send()
            whole_copy(h, k).wait_send()
        return 0

    lax.fori_loop(1, groups, end_sends, 0)
    lax.fori_loop(1, team, end_team_sends, 0)


def spread(block, axis):
    count = lax.axis_size(axis)
    return lax.all_to_all(jnp.broadcast_to(block[None], (count,) + block.shape), axis, 0, 0)


def general(raw_blocks, fir_taps, recorder_channel, pairs, table):
    windows, rows, length = raw_blocks.shape
    offset = jnp.arange(length)[None, :] - jnp.arange(length)[:, None]
    filters = jnp.where(
        (offset >= 0) & (offset < fir_taps.shape[0]),
        jnp.take(fir_taps, jnp.clip(offset, 0, fir_taps.shape[0] - 1)),
        0,
    ).astype(BF16)
    channels = recorder_channel.shape[0]
    rows_of = jnp.zeros((channels,), jnp.int32).at[recorder_channel].set(jnp.arange(channels, dtype=jnp.int32))
    left, right = jnp.take(rows_of, pairs[:, 0]), jnp.take(rows_of, pairs[:, 1])
    bins = jnp.arange(NB)
    near = (jnp.abs(bins[:, None] - bins[None, :]) <= SMOOTH).astype(F32)
    smoother = near / jnp.sum(near, axis=0, keepdims=True)

    def one_window(total, window):
        filtered = dot(window, filters).astype(BF16)
        spectrum = dot(filtered, table[:length])
        re, im = spectrum[:, :NB], spectrum[:, NB:]
        size = jnp.sqrt(re * re + im * im)
        smoothed = jnp.dot(size, smoother, precision=lax.Precision.HIGHEST)
        scale = 1.0 / (smoothed + 0.1 * jnp.mean(size, axis=-1, keepdims=True) + 1e-06)
        whitened = jnp.concatenate([re * scale, im * scale], axis=1).astype(BF16)
        everything = spread(whitened, "chan").reshape(channels, 2 * NB)
        a = jnp.take(everything, left, axis=0).astype(F32)
        b = jnp.take(everything, right, axis=0).astype(F32)
        are, aim, bre, bim = a[:, :NB], a[:, NB:], b[:, :NB], b[:, NB:]
        return total + jnp.concatenate([are * bre + aim * bim, aim * bre - are * bim], axis=1), None

    total, _ = lax.scan(one_window, jnp.zeros((pairs.shape[0], 2 * NB), F32), raw_blocks)
    return jnp.sum(spread(total, "tm"), axis=0) / (windows * lax.axis_size("tm"))


def local(raw_blocks, fir_taps, recorder_channel, pairs):
    windows, rows, length = raw_blocks.shape
    pair_count = pairs.shape[0]
    groups, team = 16, 8
    share = pair_count // team
    table = jnp.asarray(table_values(length, 128))
    hbm = pl.BlockSpec(memory_space=pltpu.HBM)
    vmem = pl.BlockSpec(memory_space=pltpu.VMEM)
    dma = pltpu.SemaphoreType.DMA
    out, flag = pl.pallas_call(
        kernel,
        out_shape=[
            jax.ShapeDtypeStruct((pair_count, 2 * NB), BF16),
            jax.ShapeDtypeStruct((1,), F32),
        ],
        in_specs=[hbm] * 5,
        out_specs=[vmem, pl.BlockSpec(memory_space=pltpu.SMEM)],
        scratch_shapes=[
            pltpu.VMEM((windows, rows, length), BF16),
            pltpu.VMEM((1, 128), BF16),
            pltpu.VMEM((80, 128), jnp.int32),
            pltpu.VMEM((2, pair_count), jnp.int32),
            pltpu.VMEM((length + 128, 2 * NB), BF16),
            pltpu.VMEM((length, 2 * NB), BF16),
            pltpu.VMEM((2, rows, windows * NB), BF16),
            pltpu.VMEM((groups, 8, 128), F32),
            pltpu.VMEM((groups, 8, 128), F32),
            pltpu.VMEM((groups * 8, 128), F32),
            pltpu.VMEM((groups * 8, 128), F32),
            pltpu.VMEM((2, groups, 2 * CAP, 2 * NB), BF16),
            pltpu.VMEM((2, groups, 2 * CAP, 2 * NB), BF16),
            pltpu.VMEM((groups * SLOT, windows * NB), BF16),
            pltpu.VMEM((groups // 2, 128), F32),
            pltpu.VMEM((2, pair_count, groups * SLOT), BF16),
            pltpu.VMEM((2, team, share, NB), BF16),
            pltpu.VMEM((2, team, share, NB), BF16),
            pltpu.VMEM((2, team, share, NB), BF16),
            dma((windows,)),
            dma((4,)),
            dma((groups,)),
            dma((groups,)),
            dma((2, groups)),
            dma((2, groups)),
            dma((2, team)),
            dma((2, team)),
            dma((2, team)),
            dma((2, team)),
        ],
        compiler_params=pltpu.CompilerParams(
            collective_id=0, has_side_effects=True, vmem_limit_bytes=40 * 2**20
        ),
    )(raw_blocks, fir_taps.reshape(1, -1), recorder_channel.reshape(-1, 128), pairs.T, table)
    return lax.cond(
        flag[0] > 0.0,
        lambda: general(raw_blocks, fir_taps, recorder_channel, pairs, table),
        lambda: out.astype(F32),
    )


def solution(mesh):
    in_specs = (P("tm", "chan", None), P(), P(), P("chan", None))
    out_specs = P("chan", None)
    return jax.shard_map(local, mesh=mesh, in_specs=in_specs, out_specs=out_specs, check_vma=False)
```

```python
import jax
import jax.numpy as jnp
import numpy as np
from jax import lax
from jax.experimental import pallas as pl
from jax.experimental.pallas import tpu as pltpu
from jax.sharding import PartitionSpec as P

NB = 128
SMOOTH = 4
CAP1 = 160
CAP2 = 176
SLOT = 256
MESH = pl.DeviceIdType.MESH
F32 = jnp.float32
BF16 = jnp.bfloat16
NT = (((1,), (1,)), ((), ()))


def table_values(length, extra):
    samples = np.arange(length, dtype=np.int64)
    freqs = np.arange(1, NB + 1, dtype=np.int64)
    angles = (samples[:, None] * freqs[None, :] % length).astype(np.float32) * np.float32(2.0 * np.pi / length)
    table = np.concatenate([np.cos(angles), -np.sin(angles)], axis=1)
    return np.concatenate([table, np.zeros((extra, 2 * NB), np.float32)]).astype(BF16)


def iota(shape, dim):
    return lax.broadcasted_iota(jnp.int32, shape, dim)


def dot(left, right):
    return jnp.dot(left, right, preferred_element_type=F32)


def dot_nt(left, right):
    return lax.dot_general(left, right, NT, preferred_element_type=F32)


def one(condition):
    return jnp.where(condition, 1.0, 0.0)


def ranks_of(marks, group):
    count = marks.shape[0]
    held = marks.astype(BF16)
    upto = dot(held, one(iota((128, 128), 0) <= iota((128, 128), 1)).astype(BF16))
    totals = dot(held, jnp.ones((128, 128), BF16))
    row, col = iota((count, count), 0), iota((count, count), 1)
    before = dot(one((row // group == col // group) & (col < row)).astype(BF16), totals.astype(BF16))
    return jnp.where(marks > 0.0, upto + before - 1.0, -1.0)


def row_of(ref, first):
    return jnp.concatenate([ref[pl.ds(first + k, 1), :] for k in range(5)], axis=1)


def roll_half(value):
    return pltpu.roll(value, NB // 2, 1)


def kernel(
    raw_hbm, taps_hbm, rec_hbm, pairs_hbm, table_hbm, out_ref, flag_ref,
    raw, taps, rec, pairs, table, fold, white, marks, inner, union, wanted, own_rank, inner_rank, union_rank, wanted_rank,
    pick1, pick2, send1, recv1, send2, recv2, slot, take, part, parts, whole, flags,
    load_sem, small_sem, ask1_send, ask1_recv, ask2_send, ask2_recv, hop1_send, hop1_recv, hop2_send, hop2_recv,
    part_send, part_recv, whole_send, whole_recv, flag_send, flag_recv,
):
    t, c = lax.axis_index("tm"), lax.axis_index("chan")
    first, second = (c // 4, c % 4), (c % 4, c // 4)
    windows, rows, length = raw.shape
    side = 4
    groups = side * side
    team = 8
    pair_count = out_ref.shape[0]
    share = pair_count // team

    small = [(pairs_hbm, pairs), (rec_hbm, rec), (taps_hbm, taps), (table_hbm, table)]

    def small_copy(i):
        return pltpu.make_async_copy(small[i][0], small[i][1], small_sem.at[i])

    def load_copy(w):
        return pltpu.make_async_copy(raw_hbm.at[w], raw.at[w], load_sem.at[w])

    for i in range(len(small)):
        small_copy(i).start()
    for w in range(windows):
        load_copy(w).start()

    def chan_of(o, f, s):
        return s * side + f if o else f * side + s

    barrier = pltpu.get_barrier_semaphore()
    for o in range(2):
        for k in range(1, side):
            pl.semaphore_signal(
                barrier, inc=1, device_id=(t, chan_of(o, (first[o] + k) % side, second[o])), device_id_type=MESH
            )

    def greet_tm(k, _):
        pl.semaphore_signal(barrier, inc=1, device_id=((t + k) % team, c), device_id_type=MESH)
        return 0

    lax.fori_loop(1, team, greet_tm, 0)

    small_copy(0).wait()
    ends = pairs[...]
    high, low = ends // 128, ends % 128
    place = iota((128, pair_count), 0)
    named = jnp.zeros((128, 128), F32)
    for e in range(2):
        named += dot_nt(
            one(low[e : e + 1] == place).astype(BF16), one(high[e : e + 1] == place).astype(BF16)
        )
    named = one(named > 0.0).astype(BF16)
    marks[...] = jnp.zeros_like(marks)
    recv2[...] = jnp.zeros_like(recv2)
    small_copy(1).wait()

    def mark(j, _):
        ids = jnp.concatenate([rec[pl.ds(j * 10 + k, 1), :] for k in range(10)], axis=1)
        place = iota((128, 2 * rows), 0)
        found = dot(named, one(ids // 128 == place).astype(BF16))
        line = jnp.sum(jnp.where(ids % 128 == place, found, 0.0), axis=0, keepdims=True)
        for k in range(10):
            r = j * 2 + k // 5
            bit = line[:, k * 128 : (k + 1) * 128]
            marks[1, r, pl.ds(k % 5, 1), :] = bit
            marks[0, r % side * side + r // side, pl.ds(k % 5, 1), :] = bit
        return 0

    lax.fori_loop(0, groups // 2, mark, 0)

    pl.semaphore_wait(barrier, 2 * (side - 1) + team - 1)

    def ask1(o, k):
        s = (second[o] + k) % side
        return pltpu.make_async_remote_copy(
            marks.at[o, pl.ds(s * side, side)], inner.at[o, second[o]], ask1_send.at[o, k], ask1_recv.at[o, k],
            device_id=(t, chan_of(o, first[o], s)), device_id_type=MESH,
        )

    def ask2(o, k):
        f = (first[o] + k) % side
        return pltpu.make_async_remote_copy(
            union.at[o, f], wanted.at[o, first[o]], ask2_send.at[o, k], ask2_recv.at[o, k],
            device_id=(t, chan_of(o, f, second[o])), device_id_type=MESH,
        )

    for k in (2, 1, 3):
        for o in range(2):
            ask1(o, k).start()
    for o in range(2):
        inner[o, pl.ds(second[o], 1)] = marks[o, pl.ds(second[o] * side, side)][None]

    small_copy(2).wait()
    shifted = jnp.broadcast_to(
        jnp.concatenate([taps[...].astype(F32), jnp.zeros((1, 128), F32)], axis=1), (128, 256)
    )
    line = iota((128, 256), 0)
    for bit in range(7):
        shifted = jnp.where((line // (1 << bit)) % 2 == 1, pltpu.roll(shifted, 1 << bit, 1), shifted)
    block = shifted.astype(BF16)
    small_copy(3).wait()
    for k in range(length // 128):
        fold[pl.ds(k * 128, 128), :] = dot(block, table[pl.ds(k * 128, 256), :]).astype(BF16)

    bins = iota((1, NB), 1)
    inv_count = 1.0 / (
        jnp.minimum(bins + SMOOTH, NB - 1) - jnp.maximum(bins - SMOOTH, 0) + 1
    ).astype(F32)
    from_bin, to_bin = iota((2 * NB, 2 * NB), 0) % NB, iota((2 * NB, 2 * NB), 1)
    near = (from_bin - to_bin <= SMOOTH) & (to_bin - from_bin <= SMOOTH)
    band = one(near | (to_bin >= NB)).astype(BF16)
    lower = iota((rows // 2, NB), 1) < NB // 2

    def whiten(w):
        load_copy(w).wait()
        for half in range(2):
            here = pl.ds(half * (rows // 2), rows // 2)
            spectrum = dot(raw[w, here, :], fold[...])
            re, im = spectrum[:, :NB], spectrum[:, NB:]
            size = jnp.sqrt(re * re + im * im)
            big = size.astype(BF16)
            rest = (size - big.astype(F32)).astype(BF16)
            sums = dot(jnp.concatenate([big, rest], axis=1), band)
            scale = 1.0 / (sums[:, :NB] * inv_count + sums[:, NB:] * (0.1 / NB) + 1e-06)
            re, im = re * scale, im * scale
            lanes = pl.ds(w * NB, NB)
            white[0, here, lanes] = jnp.where(lower, re, roll_half(im)).astype(BF16)
            white[1, here, lanes] = jnp.where(lower, roll_half(re), im).astype(BF16)

    whiten(0)
    whiten(1)
    for o in range(2):
        for k in range(1, side):
            ask1(o, k).wait_recv()
    for o in range(2):
        either = inner[o, 0]
        for ps in range(1, side):
            either += inner[o, ps]
        union[o] = one(either > 0.0)
    for k in (2, 1, 3):
        for o in range(2):
            ask2(o, k).start()
    for o in range(2):
        wanted[o, pl.ds(first[o], 1)] = union[o, pl.ds(first[o], 1)]
    whiten(2)
    whiten(3)
    ranks = ranks_of(inner[...].reshape(2 * groups * 8, 128), side * 8)
    inner_rank[...] = ranks
    over = jnp.max(one(ranks >= CAP2), axis=0, keepdims=True)
    ranks = ranks_of(union[...].reshape(2 * side * 8, 128), 8)
    union_rank[...] = ranks
    over = jnp.maximum(over, jnp.max(one(ranks >= CAP1), axis=0, keepdims=True))
    flags[0, 0] = jnp.broadcast_to(over, (8, 128))
    for o in range(2):
        for k in range(1, side):
            ask2(o, k).wait_recv()
    wanted_rank[...] = ranks_of(wanted[...].reshape(2 * side * 8, 128), 8)

    def hop1(o, h, k):
        f = (first[o] + k) % side
        return pltpu.make_async_remote_copy(
            send1.at[o, h, f], recv1.at[o, h, first[o]], hop1_send.at[o, h, k], hop1_recv.at[o, h, k],
            device_id=(t, chan_of(o, f, second[o])), device_id_type=MESH,
        )

    def hop2(o, h, k):
        s = (second[o] + k) % side
        return pltpu.make_async_remote_copy(
            send2.at[o, h, s], recv2.at[o, h, second[o], pl.ds(0, CAP2)], hop2_send.at[o, h, k], hop2_recv.at[o, h, k],
            device_id=(t, chan_of(o, first[o], s)), device_id_type=MESH,
        )

    def flag_copy(o, k):
        to = chan_of(o, (first[o] + k) % side, second[o])
        return pltpu.make_async_remote_copy(
            flags.at[o, 0], flags.at[o, k], flag_send.at[o, k], flag_recv.at[o, k],
            device_id=(t, to), device_id_type=MESH,
        )

    for h in range(2):
        for o in range(2):
            if h == 0:
                for pf in range(side):
                    ranked = row_of(wanted_rank, o * side * 8 + pf * 8)
                    pick1[o, pl.ds(pf * CAP1, CAP1), :] = one(
                        ranked == iota((CAP1, rows), 0).astype(F32)
                    ).astype(BF16)
            lanes = pl.ds(o * 2 * NB, 2 * NB)
            send1[o, h] = dot(pick1[o], white[h, :, lanes]).astype(BF16).reshape(side, CAP1, 2 * NB)
            for k in (2, 1, 3):
                hop1(o, h, k).start()
            recv1[o, h, pl.ds(first[o], 1)] = send1[o, h, pl.ds(first[o], 1)]
    for k in range(1, side):
        flag_copy(0, k).start()

    for o in range(2):

        def cross_over(rf, _, o=o):
            into = one(
                row_of(union_rank, o * side * 8 + rf * 8) == iota((CAP1, rows), 0).astype(F32)
            ).astype(BF16)
            for ps in range(side):
                out = one(
                    row_of(inner_rank, o * groups * 8 + ps * side * 8 + rf * 8) == iota((CAP2, rows), 0).astype(F32)
                ).astype(BF16)
                pick2[o, rf, pl.ds(ps * CAP2, CAP2), :] = dot_nt(out, into).astype(BF16)
            return 0

        lax.fori_loop(0, side, cross_over, 0)

    def forward(h):
        for o in range(2):
            for k in range(1, side):
                hop1(o, h, k).wait_recv()
            total = dot(pick2[o, 0], recv1[o, h, 0])
            for rf in range(1, side):
                total += dot(pick2[o, rf], recv1[o, h, rf])
            send2[o, h] = total.astype(BF16).reshape(side, CAP2, 2 * NB)
            for k in (2, 1, 3):
                hop2(o, h, k).start()
            recv2[o, h, pl.ds(second[o], 1), pl.ds(0, CAP2)] = send2[o, h, pl.ds(second[o], 1)]

    forward(0)
    ranks = ranks_of(marks[...].reshape(2 * groups * 8, 128), side * 8)
    own_rank[...] = jnp.where(ranks < CAP2, ranks, -1.0)

    columns = jnp.concatenate([ends.astype(F32), jnp.zeros((6, pair_count), F32)], axis=0).T

    def name_slots(o):
        def name_line(rs, _):
            found = jnp.zeros((8, SLOT), F32)
            for rf in range(side):
                ids = row_of(rec, chan_of(o, rf, rs) * 5)
                ranked = row_of(own_rank, o * groups * 8 + rs * side * 8 + rf * 8)
                chosen = one(ranked == iota((SLOT, rows), 0).astype(F32)).astype(BF16)
                kind = iota((8, rows), 0)
                values = jnp.where(
                    kind == 0, (ids // 128).astype(F32), jnp.where(kind == 1, (ids % 128).astype(F32), 1.0)
                )
                found += dot_nt(values.astype(BF16), chosen)
            slot[pl.ds(o * side + rs, 1), :] = jnp.where(
                found[2:3] > 0.0, found[0:1] * 128.0 + found[1:2], -1.0
            )
            return 0

        lax.fori_loop(0, side, name_line, 0)
        for e in range(2):
            for rs in range(side):
                take[o, e, :, rs * SLOT : (rs + 1) * SLOT] = one(
                    columns[:, e : e + 1] == slot[o * side + rs : o * side + rs + 1, :]
                ).astype(BF16)

    name_slots(0)
    forward(1)
    name_slots(1)
    for k in range(1, side):
        flag_copy(0, k).wait_recv()
    flags[1, 0] = jnp.max(flags[0], axis=0)
    for k in range(1, side):
        flag_copy(1, k).start()

    def part_copy(h, to, source):
        return pltpu.make_async_remote_copy(
            part.at[h, to], parts.at[h, source], part_send.at[h, to], part_recv.at[h, source],
            device_id=(to, c), device_id_type=MESH,
        )

    def whole_copy(h, k):
        return pltpu.make_async_remote_copy(
            whole.at[h, t], whole.at[h, t], whole_send.at[h, k], whole_recv.at[h, k],
            device_id=((t + k) % team, c), device_id_type=MESH,
        )

    def add_parts(h):
        def end_part(k, _):
            part_copy(h, 0, (t + k) % team).wait_recv()
            return 0

        def start_whole(k, _):
            whole_copy(h, k).start()
            return 0

        parts[h, pl.ds(t, 1)] = part[h, pl.ds(t, 1)]
        lax.fori_loop(1, team, end_part, 0)
        whole[h, pl.ds(t, 1)] = jnp.sum(parts[h].astype(F32), axis=0, keepdims=True).astype(BF16)
        lax.fori_loop(1, team, start_whole, 0)

    for h in range(2):
        for o in range(2):
            for k in range(1, side):
                hop2(o, h, k).wait_recv()
        if h:
            add_parts(0)
        for q in range(2):
            some = pl.ds(q * (pair_count // 2), pair_count // 2)
            straight = jnp.zeros((pair_count // 2, NB), F32)
            crossed = jnp.zeros((pair_count // 2, NB), F32)
            for o in range(2):
                arrived = recv2[o, h].reshape(side * SLOT, 2 * NB)
                a = dot(take[o, 0, some, :], arrived)
                b = dot(take[o, 1, some, :], arrived)
                for w in range(2):
                    aw, bw = a[:, w * NB : (w + 1) * NB], b[:, w * NB : (w + 1) * NB]
                    straight += aw * bw
                    crossed += aw * roll_half(bw)
            lower = iota((pair_count // 2, NB), 1) < NB // 2
            product = jnp.where(lower, straight + roll_half(straight), crossed - roll_half(crossed))
            part[h, pl.ds(q * (team // 2), team // 2)] = (
                (product * (1.0 / (windows * team))).astype(BF16).reshape(team // 2, share, NB)
            )

            def start_part(k, _, h=h):
                @pl.when(k != t)
                def _():
                    part_copy(h, k, t).start()

                return 0

            lax.fori_loop(q * (team // 2), (q + 1) * (team // 2), start_part, 0)
    add_parts(1)

    def end_whole(k, _):
        for h in range(2):
            whole_copy(h, k).wait_recv()
        return 0

    lax.fori_loop(1, team, end_whole, 0)
    near_bins = whole[0].astype(F32).reshape(pair_count, NB)
    far_bins = whole[1].astype(F32).reshape(pair_count, NB)
    lower = iota((pair_count, NB), 1) < NB // 2
    out_ref[:, :NB] = jnp.where(lower, near_bins, roll_half(far_bins)).astype(BF16)
    out_ref[:, NB:] = jnp.where(lower, roll_half(near_bins), far_bins).astype(BF16)
    for k in range(1, side):
        flag_copy(1, k).wait_recv()
    flag_ref[0] = jnp.max(flags[1])

    for o in range(2):
        for k in range(1, side):
            ask1(o, k).wait_send()
            ask2(o, k).wait_send()
            flag_copy(o, k).wait_send()
            for h in range(2):
                hop1(o, h, k).wait_send()
                hop2(o, h, k).wait_send()

    def end_team_sends(k, _):
        for h in range(2):
            part_copy(h, (t + k) % team, t).wait_send()
            whole_copy(h, k).wait_send()
        return 0

    lax.fori_loop(1, team, end_team_sends, 0)


def spread(block, axis):
    count = lax.axis_size(axis)
    return lax.all_to_all(jnp.broadcast_to(block[None], (count,) + block.shape), axis, 0, 0)


def general(raw_blocks, fir_taps, recorder_channel, pairs, table):
    windows, rows, length = raw_blocks.shape
    offset = jnp.arange(length)[None, :] - jnp.arange(length)[:, None]
    filters = jnp.where(
        (offset >= 0) & (offset < fir_taps.shape[0]),
        jnp.take(fir_taps, jnp.clip(offset, 0, fir_taps.shape[0] - 1)),
        0,
    ).astype(BF16)
    channels = recorder_channel.shape[0]
    rows_of = jnp.zeros((channels,), jnp.int32).at[recorder_channel].set(jnp.arange(channels, dtype=jnp.int32))
    left, right = jnp.take(rows_of, pairs[:, 0]), jnp.take(rows_of, pairs[:, 1])
    bins = jnp.arange(NB)
    near = (jnp.abs(bins[:, None] - bins[None, :]) <= SMOOTH).astype(F32)
    smoother = near / jnp.sum(near, axis=0, keepdims=True)

    def one_window(total, window):
        filtered = dot(window, filters).astype(BF16)
        spectrum = dot(filtered, table[:length])
        re, im = spectrum[:, :NB], spectrum[:, NB:]
        size = jnp.sqrt(re * re + im * im)
        smoothed = jnp.dot(size, smoother, precision=lax.Precision.HIGHEST)
        scale = 1.0 / (smoothed + 0.1 * jnp.mean(size, axis=-1, keepdims=True) + 1e-06)
        whitened = jnp.concatenate([re * scale, im * scale], axis=1).astype(BF16)
        everything = spread(whitened, "chan").reshape(channels, 2 * NB)
        a = jnp.take(everything, left, axis=0).astype(F32)
        b = jnp.take(everything, right, axis=0).astype(F32)
        are, aim, bre, bim = a[:, :NB], a[:, NB:], b[:, :NB], b[:, NB:]
        return total + jnp.concatenate([are * bre + aim * bim, aim * bre - are * bim], axis=1), None

    total, _ = lax.scan(one_window, jnp.zeros((pairs.shape[0], 2 * NB), F32), raw_blocks)
    return jnp.sum(spread(total, "tm"), axis=0) / (windows * lax.axis_size("tm"))


def local(raw_blocks, fir_taps, recorder_channel, pairs):
    windows, rows, length = raw_blocks.shape
    pair_count = pairs.shape[0]
    side, groups, team = 4, 16, 8
    share = pair_count // team
    table = jnp.asarray(table_values(length, 128))
    hbm = pl.BlockSpec(memory_space=pltpu.HBM)
    vmem = pl.BlockSpec(memory_space=pltpu.VMEM)
    dma = pltpu.SemaphoreType.DMA
    out, flag = pl.pallas_call(
        kernel,
        out_shape=[
            jax.ShapeDtypeStruct((pair_count, 2 * NB), BF16),
            jax.ShapeDtypeStruct((1,), F32),
        ],
        in_specs=[hbm] * 5,
        out_specs=[vmem, pl.BlockSpec(memory_space=pltpu.SMEM)],
        scratch_shapes=[
            pltpu.VMEM((windows, rows, length), BF16),
            pltpu.VMEM((1, 128), BF16),
            pltpu.VMEM((80, 128), jnp.int32),
            pltpu.VMEM((2, pair_count), jnp.int32),
            pltpu.VMEM((length + 128, 2 * NB), BF16),
            pltpu.VMEM((length, 2 * NB), BF16),
            pltpu.VMEM((2, rows, windows * NB), BF16),
            pltpu.VMEM((2, groups, 8, 128), F32),
            pltpu.VMEM((2, side, side, 8, 128), F32),
            pltpu.VMEM((2, side, 8, 128), F32),
            pltpu.VMEM((2, side, 8, 128), F32),
            pltpu.VMEM((2 * groups * 8, 128), F32),
            pltpu.VMEM((2 * groups * 8, 128), F32),
            pltpu.VMEM((2 * side * 8, 128), F32),
            pltpu.VMEM((2 * side * 8, 128), F32),
            pltpu.VMEM((2, side * CAP1, rows), BF16),
            pltpu.VMEM((2, side, side * CAP2, CAP1), BF16),
            pltpu.VMEM((2, 2, side, CAP1, 2 * NB), BF16),
            pltpu.VMEM((2, 2, side, CAP1, 2 * NB), BF16),
            pltpu.VMEM((2, 2, side, CAP2, 2 * NB), BF16),
            pltpu.VMEM((2, 2, side, SLOT, 2 * NB), BF16),
            pltpu.VMEM((2 * side, SLOT), F32),
            pltpu.VMEM((2, 2, pair_count, side * SLOT), BF16),
            pltpu.VMEM((2, team, share, NB), BF16),
            pltpu.VMEM((2, team, share, NB), BF16),
            pltpu.VMEM((2, team, share, NB), BF16),
            pltpu.VMEM((2, side, 8, 128), F32),
            dma((windows,)),
            dma((4,)),
            dma((2, side)),
            dma((2, side)),
            dma((2, side)),
            dma((2, side)),
            dma((2, 2, side)),
            dma((2, 2, side)),
            dma((2, 2, side)),
            dma((2, 2, side)),
            dma((2, team)),
            dma((2, team)),
            dma((2, team)),
            dma((2, team)),
            dma((2, side)),
            dma((2, side)),
        ],
        compiler_params=pltpu.CompilerParams(
            collective_id=0, has_side_effects=True, vmem_limit_bytes=40 * 2**20
        ),
    )(raw_blocks, fir_taps.reshape(1, -1), recorder_channel.reshape(-1, 128), pairs.T, table)
    return lax.cond(
        flag[0] > 0.0,
        lambda: general(raw_blocks, fir_taps, recorder_channel, pairs, table),
        lambda: out.astype(F32),
    )


def solution(mesh):
    in_specs = (P("tm", "chan", None), P(), P(), P("chan", None))
    out_specs = P("chan", None)
    return jax.shard_map(local, mesh=mesh, in_specs=in_specs, out_specs=out_specs, check_vma=False)
```

```python
import jax
import jax.numpy as jnp
import numpy as np
from jax import lax
from jax.experimental import pallas as pl
from jax.experimental.pallas import tpu as pltpu
from jax.sharding import PartitionSpec as P

NB = 128
SMOOTH = 4
CAP1 = 160
CAP2 = 176
SLOT = 256
MESH = pl.DeviceIdType.MESH
F32 = jnp.float32
BF16 = jnp.bfloat16
NT = (((1,), (1,)), ((), ()))


def table_values(length, extra):
    samples = np.arange(length, dtype=np.int64)
    freqs = np.arange(1, NB + 1, dtype=np.int64)
    angles = (samples[:, None] * freqs[None, :] % length).astype(np.float32) * np.float32(2.0 * np.pi / length)
    table = np.concatenate([np.cos(angles), -np.sin(angles)], axis=1)
    return np.concatenate([table, np.zeros((extra, 2 * NB), np.float32)]).astype(BF16)


def iota(shape, dim):
    return lax.broadcasted_iota(jnp.int32, shape, dim)


def dot(left, right):
    return jnp.dot(left, right, preferred_element_type=F32)


def dot_nt(left, right):
    return lax.dot_general(left, right, NT, preferred_element_type=F32)


def one(condition):
    return jnp.where(condition, 1.0, 0.0)


def ranks_of(marks, group):
    count = marks.shape[0]
    held = marks.astype(BF16)
    upto = dot(held, one(iota((128, 128), 0) <= iota((128, 128), 1)).astype(BF16))
    totals = dot(held, jnp.ones((128, 128), BF16))
    row, col = iota((count, count), 0), iota((count, count), 1)
    before = dot(one((row // group == col // group) & (col < row)).astype(BF16), totals.astype(BF16))
    return jnp.where(marks > 0.0, upto + before - 1.0, -1.0)


def row_of(ref, first):
    return jnp.concatenate([ref[pl.ds(first + k, 1), :] for k in range(5)], axis=1)


def roll_half(value):
    return pltpu.roll(value, NB // 2, 1)


def kernel(
    raw_hbm, taps_hbm, rec_hbm, pairs_hbm, table_hbm, out_ref, flag_ref,
    raw, taps, rec, pairs, table, fold, white, marks, inner, union, wanted, own_rank, inner_rank, union_rank, wanted_rank,
    pick1, pick2, send1, recv1, send2, recv2, slot, take, part, parts, whole, flags,
    load_sem, small_sem, ask1_send, ask1_recv, ask2_send, ask2_recv, hop1_send, hop1_recv, hop2_send, hop2_recv,
    part_send, part_recv, whole_send, whole_recv, flag_send, flag_recv,
):
    t, c = lax.axis_index("tm"), lax.axis_index("chan")
    first, second = (c // 4, c % 4), (c % 4, c // 4)
    windows, rows, length = raw.shape
    side = 4
    groups = side * side
    team = 8
    pair_count = out_ref.shape[0]
    share = pair_count // team

    small = [(pairs_hbm, pairs), (rec_hbm, rec), (taps_hbm, taps), (table_hbm, table)]

    def small_copy(i):
        return pltpu.make_async_copy(small[i][0], small[i][1], small_sem.at[i])

    def load_copy(w):
        return pltpu.make_async_copy(raw_hbm.at[w], raw.at[w], load_sem.at[w])

    for i in range(len(small)):
        small_copy(i).start()
    for w in range(windows):
        load_copy(w).start()

    def chan_of(o, f, s):
        return s * side + f if o else f * side + s

    barrier = pltpu.get_barrier_semaphore()
    for o in range(2):
        for k in range(1, side):
            pl.semaphore_signal(
                barrier, inc=1, device_id=(t, chan_of(o, (first[o] + k) % side, second[o])), device_id_type=MESH
            )

    def greet_tm(k, _):
        pl.semaphore_signal(barrier, inc=1, device_id=((t + k) % team, c), device_id_type=MESH)
        return 0

    lax.fori_loop(1, team, greet_tm, 0)

    small_copy(0).wait()
    ends = pairs[...]
    high, low = ends // 128, ends % 128
    place = iota((128, pair_count), 0)
    named = jnp.zeros((128, 128), F32)
    for e in range(2):
        named += dot_nt(
            one(low[e : e + 1] == place).astype(BF16), one(high[e : e + 1] == place).astype(BF16)
        )
    named = one(named > 0.0).astype(BF16)
    marks[...] = jnp.zeros_like(marks)
    recv2[...] = jnp.zeros_like(recv2)
    slot[...] = jnp.full_like(slot, -1.0)
    small_copy(1).wait()

    def mark(j, _):
        ids = jnp.concatenate([rec[pl.ds(j * 10 + k, 1), :] for k in range(10)], axis=1)
        place = iota((128, 2 * rows), 0)
        found = dot(named, one(ids // 128 == place).astype(BF16))
        line = jnp.sum(jnp.where(ids % 128 == place, found, 0.0), axis=0, keepdims=True)
        for k in range(10):
            r = j * 2 + k // 5
            bit = line[:, k * 128 : (k + 1) * 128]
            marks[1, r, pl.ds(k % 5, 1), :] = bit
            marks[0, r % side * side + r // side, pl.ds(k % 5, 1), :] = bit
        return 0

    lax.fori_loop(0, groups // 2, mark, 0)

    pl.semaphore_wait(barrier, 2 * (side - 1) + team - 1)

    def ask1(o, k):
        s = (second[o] + k) % side
        return pltpu.make_async_remote_copy(
            marks.at[o, pl.ds(s * side, side)], inner.at[o, second[o]], ask1_send.at[o, k], ask1_recv.at[o, k],
            device_id=(t, chan_of(o, first[o], s)), device_id_type=MESH,
        )

    def ask2(o, k):
        f = (first[o] + k) % side
        return pltpu.make_async_remote_copy(
            union.at[o, f], wanted.at[o, first[o]], ask2_send.at[o, k], ask2_recv.at[o, k],
            device_id=(t, chan_of(o, f, second[o])), device_id_type=MESH,
        )

    for k in (2, 1, 3):
        for o in range(2):
            ask1(o, k).start()
    for o in range(2):
        inner[o, pl.ds(second[o], 1)] = marks[o, pl.ds(second[o] * side, side)][None]

    small_copy(2).wait()
    shifted = jnp.broadcast_to(
        jnp.concatenate([taps[...].astype(F32), jnp.zeros((1, 128), F32)], axis=1), (128, 256)
    )
    line = iota((128, 256), 0)
    for bit in range(7):
        shifted = jnp.where((line // (1 << bit)) % 2 == 1, pltpu.roll(shifted, 1 << bit, 1), shifted)
    block = shifted.astype(BF16)
    small_copy(3).wait()
    for k in range(length // 128):
        fold[pl.ds(k * 128, 128), :] = dot(block, table[pl.ds(k * 128, 256), :]).astype(BF16)

    bins = iota((1, NB), 1)
    inv_count = 1.0 / (
        jnp.minimum(bins + SMOOTH, NB - 1) - jnp.maximum(bins - SMOOTH, 0) + 1
    ).astype(F32)
    from_bin, to_bin = iota((2 * NB, 2 * NB), 0) % NB, iota((2 * NB, 2 * NB), 1)
    near = (from_bin - to_bin <= SMOOTH) & (to_bin - from_bin <= SMOOTH)
    band = one(near | (to_bin >= NB)).astype(BF16)
    lower = iota((rows // 2, NB), 1) < NB // 2

    def whiten(w):
        load_copy(w).wait()
        for half in range(2):
            here = pl.ds(half * (rows // 2), rows // 2)
            spectrum = dot(raw[w, here, :], fold[...])
            re, im = spectrum[:, :NB], spectrum[:, NB:]
            size = jnp.sqrt(re * re + im * im)
            big = size.astype(BF16)
            rest = (size - big.astype(F32)).astype(BF16)
            sums = dot(jnp.concatenate([big, rest], axis=1), band)
            scale = 1.0 / (sums[:, :NB] * inv_count + sums[:, NB:] * (0.1 / NB) + 1e-06)
            re, im = re * scale, im * scale
            lanes = pl.ds(w * NB, NB)
            white[0, here, lanes] = jnp.where(lower, re, roll_half(im)).astype(BF16)
            white[1, here, lanes] = jnp.where(lower, roll_half(re), im).astype(BF16)

    whiten(0)
    whiten(1)
    owned = ranks_of(marks[...].reshape(2 * groups * 8, 128), side * 8)
    own_rank[...] = jnp.where(owned < CAP2, owned, -1.0)
    for o in range(2):
        for k in range(1, side):
            ask1(o, k).wait_recv()
    for o in range(2):
        either = inner[o, 0]
        for ps in range(1, side):
            either += inner[o, ps]
        union[o] = one(either > 0.0)
    for k in (2, 1, 3):
        for o in range(2):
            ask2(o, k).start()
    for o in range(2):
        wanted[o, pl.ds(first[o], 1)] = union[o, pl.ds(first[o], 1)]
    whiten(2)
    whiten(3)
    ranks = ranks_of(inner[...].reshape(2 * groups * 8, 128), side * 8)
    inner_rank[...] = ranks
    over = jnp.max(one(ranks >= CAP2), axis=0, keepdims=True)
    ranks = ranks_of(union[...].reshape(2 * side * 8, 128), 8)
    union_rank[...] = ranks
    over = jnp.maximum(over, jnp.max(one(ranks >= CAP1), axis=0, keepdims=True))
    flags[0, 0] = jnp.broadcast_to(over, (8, 128))
    for o in range(2):
        for k in range(1, side):
            ask2(o, k).wait_recv()
    wanted_rank[...] = ranks_of(wanted[...].reshape(2 * side * 8, 128), 8)

    def hop1(o, h, k):
        f = (first[o] + k) % side
        return pltpu.make_async_remote_copy(
            send1.at[o, h, f], recv1.at[o, h, first[o]], hop1_send.at[o, h, k], hop1_recv.at[o, h, k],
            device_id=(t, chan_of(o, f, second[o])), device_id_type=MESH,
        )

    def hop2(o, h, k):
        s = (second[o] + k) % side
        return pltpu.make_async_remote_copy(
            send2.at[o, h, s], recv2.at[o, h, second[o], pl.ds(0, CAP2)], hop2_send.at[o, h, k], hop2_recv.at[o, h, k],
            device_id=(t, chan_of(o, first[o], s)), device_id_type=MESH,
        )

    def flag_copy(o, k):
        to = chan_of(o, (first[o] + k) % side, second[o])
        return pltpu.make_async_remote_copy(
            flags.at[o, 0], flags.at[o, k], flag_send.at[o, k], flag_recv.at[o, k],
            device_id=(t, to), device_id_type=MESH,
        )

    for h in range(2):
        for o in range(2):
            if h == 0:
                for pf in range(side):
                    ranked = row_of(wanted_rank, o * side * 8 + pf * 8)
                    pick1[o, pl.ds(pf * CAP1, CAP1), :] = one(
                        ranked == iota((CAP1, rows), 0).astype(F32)
                    ).astype(BF16)
            lanes = pl.ds(o * 2 * NB, 2 * NB)
            send1[o, h] = dot(pick1[o], white[h, :, lanes]).astype(BF16).reshape(side, CAP1, 2 * NB)
            for k in (2, 1, 3):
                hop1(o, h, k).start()
            recv1[o, h, pl.ds(first[o], 1)] = send1[o, h, pl.ds(first[o], 1)]
    for k in range(1, side):
        flag_copy(0, k).start()

    for o in range(2):

        def cross_over(rf, _, o=o):
            into = one(
                row_of(union_rank, o * side * 8 + rf * 8) == iota((CAP1, rows), 0).astype(F32)
            ).astype(BF16)
            out = [
                one(row_of(inner_rank, o * groups * 8 + ps * side * 8 + rf * 8) == iota((CAP2, rows), 0).astype(F32))
                for ps in range(side)
            ]
            pick2[o, pl.ds(rf, 1)] = dot_nt(jnp.concatenate(out, axis=0).astype(BF16), into).astype(BF16)[None]
            return 0

        lax.fori_loop(0, side, cross_over, 0)

    columns = jnp.concatenate([ends.astype(F32), jnp.zeros((6, pair_count), F32)], axis=0).T

    def name_slots(o):
        def name_line(rs, _):
            found = jnp.zeros((8, CAP2), F32)
            for rf in range(side):
                ids = row_of(rec, chan_of(o, rf, rs) * 5)
                ranked = row_of(own_rank, o * groups * 8 + rs * side * 8 + rf * 8)
                chosen = one(ranked == iota((CAP2, rows), 0).astype(F32)).astype(BF16)
                kind = iota((8, rows), 0)
                values = jnp.where(
                    kind == 0, (ids // 128).astype(F32), jnp.where(kind == 1, (ids % 128).astype(F32), 1.0)
                )
                found += dot_nt(values.astype(BF16), chosen)
            slot[pl.ds(o * side + rs, 1), pl.ds(0, CAP2)] = jnp.where(
                found[2:3] > 0.0, found[0:1] * 128.0 + found[1:2], -1.0
            )
            return 0

        lax.fori_loop(0, side, name_line, 0)
        for e in range(2):
            for rs in range(side):
                take[o, e, :, rs * SLOT : (rs + 1) * SLOT] = one(
                    columns[:, e : e + 1] == slot[o * side + rs : o * side + rs + 1, :]
                ).astype(BF16)

    def forward(h):
        for o in range(2):
            for k in range(1, side):
                hop1(o, h, k).wait_recv()
            total = dot(pick2[o, 0], recv1[o, h, 0])
            for rf in range(1, side):
                total += dot(pick2[o, rf], recv1[o, h, rf])
            send2[o, h] = total.astype(BF16).reshape(side, CAP2, 2 * NB)
            for k in (2, 1, 3):
                hop2(o, h, k).start()
            recv2[o, h, pl.ds(second[o], 1), pl.ds(0, CAP2)] = send2[o, h, pl.ds(second[o], 1)]

    forward(0)
    name_slots(0)
    forward(1)
    name_slots(1)
    for k in range(1, side):
        flag_copy(0, k).wait_recv()
    flags[1, 0] = jnp.max(flags[0], axis=0)
    for k in range(1, side):
        flag_copy(1, k).start()

    def part_copy(h, to, source):
        return pltpu.make_async_remote_copy(
            part.at[h, to], parts.at[h, source], part_send.at[h, to], part_recv.at[h, source],
            device_id=(to, c), device_id_type=MESH,
        )

    def whole_copy(h, k):
        return pltpu.make_async_remote_copy(
            whole.at[h, t], whole.at[h, t], whole_send.at[h, k], whole_recv.at[h, k],
            device_id=((t + k) % team, c), device_id_type=MESH,
        )

    def add_parts(h):
        def end_part(k, _):
            part_copy(h, 0, (t + k) % team).wait_recv()
            return 0

        def start_whole(k, _):
            whole_copy(h, k).start()
            return 0

        parts[h, pl.ds(t, 1)] = part[h, pl.ds(t, 1)]
        lax.fori_loop(1, team, end_part, 0)
        whole[h, pl.ds(t, 1)] = jnp.sum(parts[h].astype(F32), axis=0, keepdims=True).astype(BF16)
        lax.fori_loop(1, team, start_whole, 0)

    for h in range(2):
        for o in range(2):
            for k in range(1, side):
                hop2(o, h, k).wait_recv()
        for q in range(2):
            some = pl.ds(q * (pair_count // 2), pair_count // 2)
            straight = jnp.zeros((pair_count // 2, NB), F32)
            crossed = jnp.zeros((pair_count // 2, NB), F32)
            for o in range(2):
                arrived = recv2[o, h].reshape(side * SLOT, 2 * NB)
                a = dot(take[o, 0, some, :], arrived)
                b = dot(take[o, 1, some, :], arrived)
                for w in range(2):
                    aw, bw = a[:, w * NB : (w + 1) * NB], b[:, w * NB : (w + 1) * NB]
                    straight += aw * bw
                    crossed += aw * roll_half(bw)
            lower = iota((pair_count // 2, NB), 1) < NB // 2
            product = jnp.where(lower, straight + roll_half(straight), crossed - roll_half(crossed))
            part[h, pl.ds(q * (team // 2), team // 2)] = (
                (product * (1.0 / (windows * team))).astype(BF16).reshape(team // 2, share, NB)
            )

            def start_part(k, _, h=h):
                @pl.when(k != t)
                def _():
                    part_copy(h, k, t).start()

                return 0

            lax.fori_loop(q * (team // 2), (q + 1) * (team // 2), start_part, 0)
    add_parts(0)
    add_parts(1)

    def end_whole(k, _):
        for h in range(2):
            whole_copy(h, k).wait_recv()
        return 0

    lax.fori_loop(1, team, end_whole, 0)
    near_bins = whole[0].astype(F32).reshape(pair_count, NB)
    far_bins = whole[1].astype(F32).reshape(pair_count, NB)
    lower = iota((pair_count, NB), 1) < NB // 2
    out_ref[:, :NB] = jnp.where(lower, near_bins, roll_half(far_bins)).astype(BF16)
    out_ref[:, NB:] = jnp.where(lower, roll_half(near_bins), far_bins).astype(BF16)
    for k in range(1, side):
        flag_copy(1, k).wait_recv()
    flag_ref[0] = jnp.max(flags[1])

    for o in range(2):
        for k in range(1, side):
            ask1(o, k).wait_send()
            ask2(o, k).wait_send()
            flag_copy(o, k).wait_send()
            for h in range(2):
                hop1(o, h, k).wait_send()
                hop2(o, h, k).wait_send()

    def end_team_sends(k, _):
        for h in range(2):
            part_copy(h, (t + k) % team, t).wait_send()
            whole_copy(h, k).wait_send()
        return 0

    lax.fori_loop(1, team, end_team_sends, 0)


def spread(block, axis):
    count = lax.axis_size(axis)
    return lax.all_to_all(jnp.broadcast_to(block[None], (count,) + block.shape), axis, 0, 0)


def general(raw_blocks, fir_taps, recorder_channel, pairs, table):
    windows, rows, length = raw_blocks.shape
    offset = jnp.arange(length)[None, :] - jnp.arange(length)[:, None]
    filters = jnp.where(
        (offset >= 0) & (offset < fir_taps.shape[0]),
        jnp.take(fir_taps, jnp.clip(offset, 0, fir_taps.shape[0] - 1)),
        0,
    ).astype(BF16)
    channels = recorder_channel.shape[0]
    rows_of = jnp.zeros((channels,), jnp.int32).at[recorder_channel].set(jnp.arange(channels, dtype=jnp.int32))
    left, right = jnp.take(rows_of, pairs[:, 0]), jnp.take(rows_of, pairs[:, 1])
    bins = jnp.arange(NB)
    near = (jnp.abs(bins[:, None] - bins[None, :]) <= SMOOTH).astype(F32)
    smoother = near / jnp.sum(near, axis=0, keepdims=True)

    def one_window(total, window):
        filtered = dot(window, filters).astype(BF16)
        spectrum = dot(filtered, table[:length])
        re, im = spectrum[:, :NB], spectrum[:, NB:]
        size = jnp.sqrt(re * re + im * im)
        smoothed = jnp.dot(size, smoother, precision=lax.Precision.HIGHEST)
        scale = 1.0 / (smoothed + 0.1 * jnp.mean(size, axis=-1, keepdims=True) + 1e-06)
        whitened = jnp.concatenate([re * scale, im * scale], axis=1).astype(BF16)
        everything = spread(whitened, "chan").reshape(channels, 2 * NB)
        a = jnp.take(everything, left, axis=0).astype(F32)
        b = jnp.take(everything, right, axis=0).astype(F32)
        are, aim, bre, bim = a[:, :NB], a[:, NB:], b[:, :NB], b[:, NB:]
        return total + jnp.concatenate([are * bre + aim * bim, aim * bre - are * bim], axis=1), None

    total, _ = lax.scan(one_window, jnp.zeros((pairs.shape[0], 2 * NB), F32), raw_blocks)
    return jnp.sum(spread(total, "tm"), axis=0) / (windows * lax.axis_size("tm"))


def local(raw_blocks, fir_taps, recorder_channel, pairs):
    windows, rows, length = raw_blocks.shape
    pair_count = pairs.shape[0]
    side, groups, team = 4, 16, 8
    share = pair_count // team
    table = jnp.asarray(table_values(length, 128))
    hbm = pl.BlockSpec(memory_space=pltpu.HBM)
    vmem = pl.BlockSpec(memory_space=pltpu.VMEM)
    dma = pltpu.SemaphoreType.DMA
    out, flag = pl.pallas_call(
        kernel,
        out_shape=[
            jax.ShapeDtypeStruct((pair_count, 2 * NB), BF16),
            jax.ShapeDtypeStruct((1,), F32),
        ],
        in_specs=[hbm] * 5,
        out_specs=[vmem, pl.BlockSpec(memory_space=pltpu.SMEM)],
        scratch_shapes=[
            pltpu.VMEM((windows, rows, length), BF16),
            pltpu.VMEM((1, 128), BF16),
            pltpu.VMEM((80, 128), jnp.int32),
            pltpu.VMEM((2, pair_count), jnp.int32),
            pltpu.VMEM((length + 128, 2 * NB), BF16),
            pltpu.VMEM((length, 2 * NB), BF16),
            pltpu.VMEM((2, rows, windows * NB), BF16),
            pltpu.VMEM((2, groups, 8, 128), F32),
            pltpu.VMEM((2, side, side, 8, 128), F32),
            pltpu.VMEM((2, side, 8, 128), F32),
            pltpu.VMEM((2, side, 8, 128), F32),
            pltpu.VMEM((2 * groups * 8, 128), F32),
            pltpu.VMEM((2 * groups * 8, 128), F32),
            pltpu.VMEM((2 * side * 8, 128), F32),
            pltpu.VMEM((2 * side * 8, 128), F32),
            pltpu.VMEM((2, side * CAP1, rows), BF16),
            pltpu.VMEM((2, side, side * CAP2, CAP1), BF16),
            pltpu.VMEM((2, 2, side, CAP1, 2 * NB), BF16),
            pltpu.VMEM((2, 2, side, CAP1, 2 * NB), BF16),
            pltpu.VMEM((2, 2, side, CAP2, 2 * NB), BF16),
            pltpu.VMEM((2, 2, side, SLOT, 2 * NB), BF16),
            pltpu.VMEM((2 * side, SLOT), F32),
            pltpu.VMEM((2, 2, pair_count, side * SLOT), BF16),
            pltpu.VMEM((2, team, share, NB), BF16),
            pltpu.VMEM((2, team, share, NB), BF16),
            pltpu.VMEM((2, team, share, NB), BF16),
            pltpu.VMEM((2, side, 8, 128), F32),
            dma((windows,)),
            dma((4,)),
            dma((2, side)),
            dma((2, side)),
            dma((2, side)),
            dma((2, side)),
            dma((2, 2, side)),
            dma((2, 2, side)),
            dma((2, 2, side)),
            dma((2, 2, side)),
            dma((2, team)),
            dma((2, team)),
            dma((2, team)),
            dma((2, team)),
            dma((2, side)),
            dma((2, side)),
        ],
        compiler_params=pltpu.CompilerParams(
            collective_id=0, has_side_effects=True, vmem_limit_bytes=40 * 2**20
        ),
    )(raw_blocks, fir_taps.reshape(1, -1), recorder_channel.reshape(-1, 128), pairs.T, table)
    return lax.cond(
        flag[0] > 0.0,
        lambda: general(raw_blocks, fir_taps, recorder_channel, pairs, table),
        lambda: out.astype(F32),
    )


def solution(mesh):
    in_specs = (P("tm", "chan", None), P(), P(), P("chan", None))
    out_specs = P("chan", None)
    return jax.shard_map(local, mesh=mesh, in_specs=in_specs, out_specs=out_specs, check_vma=False)
```

```python
import jax
import jax.numpy as jnp
import numpy as np
from jax import lax
from jax.experimental import pallas as pl
from jax.experimental.pallas import tpu as pltpu
from jax.sharding import PartitionSpec as P

NB = 128
SMOOTH = 4
CAP1 = 160
CAP2 = 176
SLOT = 256
MESH = pl.DeviceIdType.MESH
F32 = jnp.float32
BF16 = jnp.bfloat16
NT = (((1,), (1,)), ((), ()))


def table_values(length, extra):
    samples = np.arange(length, dtype=np.int64)
    freqs = np.arange(1, NB + 1, dtype=np.int64)
    angles = (samples[:, None] * freqs[None, :] % length).astype(np.float32) * np.float32(2.0 * np.pi / length)
    table = np.concatenate([np.cos(angles), -np.sin(angles)], axis=1)
    return np.concatenate([table, np.zeros((extra, 2 * NB), np.float32)]).astype(BF16)


def iota(shape, dim):
    return lax.broadcasted_iota(jnp.int32, shape, dim)


def dot(left, right):
    return jnp.dot(left, right, preferred_element_type=F32)


def dot_nt(left, right):
    return lax.dot_general(left, right, NT, preferred_element_type=F32)


def one(condition):
    return jnp.where(condition, 1.0, 0.0)


def ranks_of(marks, group):
    count = marks.shape[0]
    held = marks.astype(BF16)
    upto = dot(held, one(iota((128, 128), 0) <= iota((128, 128), 1)).astype(BF16))
    totals = dot(held, jnp.ones((128, 128), BF16))
    row, col = iota((count, count), 0), iota((count, count), 1)
    before = dot(one((row // group == col // group) & (col < row)).astype(BF16), totals.astype(BF16))
    return jnp.where(marks > 0.0, upto + before - 1.0, -1.0)


def row_of(ref, first):
    return jnp.concatenate([ref[pl.ds(first + k, 1), :] for k in range(5)], axis=1)


def roll_half(value):
    return pltpu.roll(value, NB // 2, 1)


def kernel(
    raw_hbm, taps_hbm, rec_hbm, pairs_hbm, table_hbm, out_ref, flag_ref,
    raw, taps, rec, pairs, table, fold, white, marks, inner, union, wanted, own_rank, inner_rank, union_rank, wanted_rank,
    pick1, pick2, send1, recv1, send2, recv2, slot, take, part, parts, whole, flags,
    load_sem, small_sem, ask1_send, ask1_recv, ask2_send, ask2_recv, hop1_send, hop1_recv, hop2_send, hop2_recv,
    part_send, part_recv, whole_send, whole_recv, flag_send, flag_recv,
):
    t, c = lax.axis_index("tm"), lax.axis_index("chan")
    first, second = (c // 4, c % 4), (c % 4, c // 4)
    windows, rows, length = raw.shape
    side = 4
    groups = side * side
    team = 8
    pair_count = out_ref.shape[0]
    share = pair_count // team

    small = [(pairs_hbm, pairs), (rec_hbm, rec), (taps_hbm, taps), (table_hbm, table)]

    def small_copy(i):
        return pltpu.make_async_copy(small[i][0], small[i][1], small_sem.at[i])

    def load_copy(w):
        return pltpu.make_async_copy(raw_hbm.at[w], raw.at[w], load_sem.at[w])

    for i in range(len(small)):
        small_copy(i).start()
    for w in range(windows):
        load_copy(w).start()

    def chan_of(o, f, s):
        return s * side + f if o else f * side + s

    barrier = pltpu.get_barrier_semaphore()
    for o in range(2):
        for k in range(1, side):
            pl.semaphore_signal(
                barrier, inc=1, device_id=(t, chan_of(o, (first[o] + k) % side, second[o])), device_id_type=MESH
            )

    def greet_tm(k, _):
        pl.semaphore_signal(barrier, inc=1, device_id=((t + k) % team, c), device_id_type=MESH)
        return 0

    lax.fori_loop(1, team, greet_tm, 0)

    small_copy(0).wait()
    ends = pairs[...]
    high, low = ends // 128, ends % 128
    place = iota((128, pair_count), 0)
    named = jnp.zeros((128, 128), F32)
    for e in range(2):
        named += dot_nt(
            one(low[e : e + 1] == place).astype(BF16), one(high[e : e + 1] == place).astype(BF16)
        )
    named = one(named > 0.0).astype(BF16)
    marks[...] = jnp.zeros_like(marks)
    small_copy(1).wait()

    def mark(j, _):
        ids = jnp.concatenate([rec[pl.ds(j * 10 + k, 1), :] for k in range(10)], axis=1)
        place = iota((128, 2 * rows), 0)
        found = dot(named, one(ids // 128 == place).astype(BF16))
        line = jnp.sum(jnp.where(ids % 128 == place, found, 0.0), axis=0, keepdims=True)
        for k in range(10):
            r = j * 2 + k // 5
            bit = line[:, k * 128 : (k + 1) * 128]
            marks[1, r, pl.ds(k % 5, 1), :] = bit
            marks[0, r % side * side + r // side, pl.ds(k % 5, 1), :] = bit
        return 0

    lax.fori_loop(0, groups // 2, mark, 0, unroll=8)

    pl.semaphore_wait(barrier, 2 * (side - 1) + team - 1)

    def ask1(o, k):
        s = (second[o] + k) % side
        return pltpu.make_async_remote_copy(
            marks.at[o, pl.ds(s * side, side)], inner.at[o, second[o]], ask1_send.at[o, k], ask1_recv.at[o, k],
            device_id=(t, chan_of(o, first[o], s)), device_id_type=MESH,
        )

    def ask2(o, k):
        f = (first[o] + k) % side
        return pltpu.make_async_remote_copy(
            union.at[o, f], wanted.at[o, first[o]], ask2_send.at[o, k], ask2_recv.at[o, k],
            device_id=(t, chan_of(o, f, second[o])), device_id_type=MESH,
        )

    for k in (2, 1, 3):
        for o in range(2):
            ask1(o, k).start()
    recv2[:, :, :, CAP2:, :] = jnp.zeros((2, 2, side, SLOT - CAP2, 2 * NB), BF16)
    slot[...] = jnp.full_like(slot, -1.0)
    for o in range(2):
        inner[o, pl.ds(second[o], 1)] = marks[o, pl.ds(second[o] * side, side)][None]

    small_copy(2).wait()
    shifted = jnp.broadcast_to(
        jnp.concatenate([taps[...].astype(F32), jnp.zeros((1, 128), F32)], axis=1), (128, 256)
    )
    line = iota((128, 256), 0)
    for bit in range(7):
        shifted = jnp.where((line // (1 << bit)) % 2 == 1, pltpu.roll(shifted, 1 << bit, 1), shifted)
    block = shifted.astype(BF16)
    small_copy(3).wait()
    for k in range(length // 128):
        fold[pl.ds(k * 128, 128), :] = dot(block, table[pl.ds(k * 128, 256), :]).astype(BF16)

    bins = iota((1, NB), 1)
    inv_count = 1.0 / (
        jnp.minimum(bins + SMOOTH, NB - 1) - jnp.maximum(bins - SMOOTH, 0) + 1
    ).astype(F32)
    from_bin, to_bin = iota((2 * NB, 2 * NB), 0) % NB, iota((2 * NB, 2 * NB), 1)
    near = (from_bin - to_bin <= SMOOTH) & (to_bin - from_bin <= SMOOTH)
    band = one(near | (to_bin >= NB)).astype(BF16)
    lower = iota((rows // 2, NB), 1) < NB // 2

    def whiten(w):
        load_copy(w).wait()
        for half in range(2):
            here = pl.ds(half * (rows // 2), rows // 2)
            spectrum = dot(raw[w, here, :], fold[...])
            re, im = spectrum[:, :NB], spectrum[:, NB:]
            size = jnp.sqrt(re * re + im * im)
            big = size.astype(BF16)
            rest = (size - big.astype(F32)).astype(BF16)
            sums = dot(jnp.concatenate([big, rest], axis=1), band)
            scale = 1.0 / (sums[:, :NB] * inv_count + sums[:, NB:] * (0.1 / NB) + 1e-06)
            re, im = re * scale, im * scale
            lanes = pl.ds(w * NB, NB)
            white[0, here, lanes] = jnp.where(lower, re, roll_half(im)).astype(BF16)
            white[1, here, lanes] = jnp.where(lower, roll_half(re), im).astype(BF16)

    whiten(0)
    whiten(1)
    owned = ranks_of(marks[...].reshape(2 * groups * 8, 128), side * 8)
    own_rank[...] = jnp.where(owned < CAP2, owned, -1.0)
    for o in range(2):
        for k in range(1, side):
            ask1(o, k).wait_recv()
    for o in range(2):
        either = inner[o, 0]
        for ps in range(1, side):
            either += inner[o, ps]
        union[o] = one(either > 0.0)
    for k in (2, 1, 3):
        for o in range(2):
            ask2(o, k).start()
    for o in range(2):
        wanted[o, pl.ds(first[o], 1)] = union[o, pl.ds(first[o], 1)]
    whiten(2)
    whiten(3)
    ranks = ranks_of(inner[...].reshape(2 * groups * 8, 128), side * 8)
    inner_rank[...] = ranks
    over = jnp.max(one(ranks >= CAP2), axis=0, keepdims=True)
    ranks = ranks_of(union[...].reshape(2 * side * 8, 128), 8)
    union_rank[...] = ranks
    over = jnp.maximum(over, jnp.max(one(ranks >= CAP1), axis=0, keepdims=True))
    flags[0, 0] = jnp.broadcast_to(over, (8, 128))
    for o in range(2):
        for k in range(1, side):
            ask2(o, k).wait_recv()
    wanted_rank[...] = ranks_of(wanted[...].reshape(2 * side * 8, 128), 8)

    def hop1(o, h, k):
        f = (first[o] + k) % side
        return pltpu.make_async_remote_copy(
            send1.at[o, h, f], recv1.at[o, h, first[o]], hop1_send.at[o, h, k], hop1_recv.at[o, h, k],
            device_id=(t, chan_of(o, f, second[o])), device_id_type=MESH,
        )

    def hop2(o, h, k):
        s = (second[o] + k) % side
        return pltpu.make_async_remote_copy(
            send2.at[o, h, s], recv2.at[o, h, second[o], pl.ds(0, CAP2)], hop2_send.at[o, h, k], hop2_recv.at[o, h, k],
            device_id=(t, chan_of(o, first[o], s)), device_id_type=MESH,
        )

    def flag_copy(o, k):
        to = chan_of(o, (first[o] + k) % side, second[o])
        return pltpu.make_async_remote_copy(
            flags.at[o, 0], flags.at[o, k], flag_send.at[o, k], flag_recv.at[o, k],
            device_id=(t, to), device_id_type=MESH,
        )

    for h in range(2):
        for o in range(2):
            if h == 0:
                for pf in range(side):
                    ranked = row_of(wanted_rank, o * side * 8 + pf * 8)
                    pick1[o, pl.ds(pf * CAP1, CAP1), :] = one(
                        ranked == iota((CAP1, rows), 0).astype(F32)
                    ).astype(BF16)
            lanes = pl.ds(o * 2 * NB, 2 * NB)
            send1[o, h] = dot(pick1[o], white[h, :, lanes]).astype(BF16).reshape(side, CAP1, 2 * NB)
            for k in (2, 1, 3):
                hop1(o, h, k).start()
            recv1[o, h, pl.ds(first[o], 1)] = send1[o, h, pl.ds(first[o], 1)]
    for k in range(1, side):
        flag_copy(0, k).start()

    for o in range(2):

        def cross_over(rf, _, o=o):
            into = one(
                row_of(union_rank, o * side * 8 + rf * 8) == iota((CAP1, rows), 0).astype(F32)
            ).astype(BF16)
            out = [
                one(row_of(inner_rank, o * groups * 8 + ps * side * 8 + rf * 8) == iota((CAP2, rows), 0).astype(F32))
                for ps in range(side)
            ]
            pick2[o, pl.ds(rf, 1)] = dot_nt(jnp.concatenate(out, axis=0).astype(BF16), into).astype(BF16)[None]
            return 0

        lax.fori_loop(0, side, cross_over, 0)

    columns = jnp.concatenate([ends.astype(F32), jnp.zeros((6, pair_count), F32)], axis=0).T

    def name_slots(o):
        def name_line(rs, _):
            found = jnp.zeros((8, CAP2), F32)
            for rf in range(side):
                ids = row_of(rec, chan_of(o, rf, rs) * 5)
                ranked = row_of(own_rank, o * groups * 8 + rs * side * 8 + rf * 8)
                chosen = one(ranked == iota((CAP2, rows), 0).astype(F32)).astype(BF16)
                kind = iota((8, rows), 0)
                values = jnp.where(
                    kind == 0, (ids // 128).astype(F32), jnp.where(kind == 1, (ids % 128).astype(F32), 1.0)
                )
                found += dot_nt(values.astype(BF16), chosen)
            slot[pl.ds(o * side + rs, 1), pl.ds(0, CAP2)] = jnp.where(
                found[2:3] > 0.0, found[0:1] * 128.0 + found[1:2], -1.0
            )
            return 0

        lax.fori_loop(0, side, name_line, 0)
        for e in range(2):
            for rs in range(side):
                take[o, e, :, rs * SLOT : (rs + 1) * SLOT] = one(
                    columns[:, e : e + 1] == slot[o * side + rs : o * side + rs + 1, :]
                ).astype(BF16)

    def forward(h):
        for o in range(2):
            for k in range(1, side):
                hop1(o, h, k).wait_recv()
            total = dot(pick2[o, 0], recv1[o, h, 0])
            for rf in range(1, side):
                total += dot(pick2[o, rf], recv1[o, h, rf])
            send2[o, h] = total.astype(BF16).reshape(side, CAP2, 2 * NB)
            for k in (2, 1, 3):
                hop2(o, h, k).start()
            recv2[o, h, pl.ds(second[o], 1), pl.ds(0, CAP2)] = send2[o, h, pl.ds(second[o], 1)]

    forward(0)
    name_slots(0)
    forward(1)
    name_slots(1)
    for k in range(1, side):
        flag_copy(0, k).wait_recv()
    flags[1, 0] = jnp.max(flags[0], axis=0)
    for k in range(1, side):
        flag_copy(1, k).start()

    def part_copy(h, to, source):
        return pltpu.make_async_remote_copy(
            part.at[h, to], parts.at[h, source], part_send.at[h, to], part_recv.at[h, source],
            device_id=(to, c), device_id_type=MESH,
        )

    def whole_copy(h, k):
        return pltpu.make_async_remote_copy(
            whole.at[h, t], whole.at[h, t], whole_send.at[h, k], whole_recv.at[h, k],
            device_id=((t + k) % team, c), device_id_type=MESH,
        )

    def add_parts(h):
        def end_part(k, _):
            part_copy(h, 0, (t + k) % team).wait_recv()
            return 0

        parts[h, pl.ds(t, 1)] = part[h, pl.ds(t, 1)]
        lax.fori_loop(1, team, end_part, 0)
        whole[h, pl.ds(t, 1)] = jnp.sum(parts[h].astype(F32), axis=0, keepdims=True).astype(BF16)
        for k in (4, 5, 3, 2, 6, 7, 1):
            whole_copy(h, k).start()

    for h in range(2):
        for o in range(2):
            for k in range(1, side):
                hop2(o, h, k).wait_recv()
        for q in range(2):
            some = pl.ds(q * (pair_count // 2), pair_count // 2)
            straight = jnp.zeros((pair_count // 2, NB), F32)
            crossed = jnp.zeros((pair_count // 2, NB), F32)
            for o in range(2):
                arrived = recv2[o, h].reshape(side * SLOT, 2 * NB)
                a = dot(take[o, 0, some, :], arrived)
                b = dot(take[o, 1, some, :], arrived)
                for w in range(2):
                    aw, bw = a[:, w * NB : (w + 1) * NB], b[:, w * NB : (w + 1) * NB]
                    straight += aw * bw
                    crossed += aw * roll_half(bw)
            lower = iota((pair_count // 2, NB), 1) < NB // 2
            product = jnp.where(lower, straight + roll_half(straight), crossed - roll_half(crossed))
            part[h, pl.ds(q * (team // 2), team // 2)] = (
                (product * (1.0 / (windows * team))).astype(BF16).reshape(team // 2, share, NB)
            )

            def start_part(k, _, h=h):
                @pl.when(k != t)
                def _():
                    part_copy(h, k, t).start()

                return 0

            lax.fori_loop(q * (team // 2), (q + 1) * (team // 2), start_part, 0)
    add_parts(0)
    add_parts(1)

    def end_whole(k, _):
        for h in range(2):
            whole_copy(h, k).wait_recv()
        return 0

    lax.fori_loop(1, team, end_whole, 0)
    near_bins = whole[0].astype(F32).reshape(pair_count, NB)
    far_bins = whole[1].astype(F32).reshape(pair_count, NB)
    lower = iota((pair_count, NB), 1) < NB // 2
    out_ref[:, :NB] = jnp.where(lower, near_bins, roll_half(far_bins)).astype(BF16)
    out_ref[:, NB:] = jnp.where(lower, roll_half(near_bins), far_bins).astype(BF16)
    for k in range(1, side):
        flag_copy(1, k).wait_recv()
    flag_ref[0] = jnp.max(flags[1])

    for o in range(2):
        for k in range(1, side):
            ask1(o, k).wait_send()
            ask2(o, k).wait_send()
            flag_copy(o, k).wait_send()
            for h in range(2):
                hop1(o, h, k).wait_send()
                hop2(o, h, k).wait_send()

    def end_team_sends(k, _):
        for h in range(2):
            part_copy(h, (t + k) % team, t).wait_send()
            whole_copy(h, k).wait_send()
        return 0

    lax.fori_loop(1, team, end_team_sends, 0)


def spread(block, axis):
    count = lax.axis_size(axis)
    return lax.all_to_all(jnp.broadcast_to(block[None], (count,) + block.shape), axis, 0, 0)


def general(raw_blocks, fir_taps, recorder_channel, pairs, table):
    windows, rows, length = raw_blocks.shape
    offset = jnp.arange(length)[None, :] - jnp.arange(length)[:, None]
    filters = jnp.where(
        (offset >= 0) & (offset < fir_taps.shape[0]),
        jnp.take(fir_taps, jnp.clip(offset, 0, fir_taps.shape[0] - 1)),
        0,
    ).astype(BF16)
    channels = recorder_channel.shape[0]
    rows_of = jnp.zeros((channels,), jnp.int32).at[recorder_channel].set(jnp.arange(channels, dtype=jnp.int32))
    left, right = jnp.take(rows_of, pairs[:, 0]), jnp.take(rows_of, pairs[:, 1])
    bins = jnp.arange(NB)
    near = (jnp.abs(bins[:, None] - bins[None, :]) <= SMOOTH).astype(F32)
    smoother = near / jnp.sum(near, axis=0, keepdims=True)

    def one_window(total, window):
        filtered = dot(window, filters).astype(BF16)
        spectrum = dot(filtered, table[:length])
        re, im = spectrum[:, :NB], spectrum[:, NB:]
        size = jnp.sqrt(re * re + im * im)
        smoothed = jnp.dot(size, smoother, precision=lax.Precision.HIGHEST)
        scale = 1.0 / (smoothed + 0.1 * jnp.mean(size, axis=-1, keepdims=True) + 1e-06)
        whitened = jnp.concatenate([re * scale, im * scale], axis=1).astype(BF16)
        everything = spread(whitened, "chan").reshape(channels, 2 * NB)
        a = jnp.take(everything, left, axis=0).astype(F32)
        b = jnp.take(everything, right, axis=0).astype(F32)
        are, aim, bre, bim = a[:, :NB], a[:, NB:], b[:, :NB], b[:, NB:]
        return total + jnp.concatenate([are * bre + aim * bim, aim * bre - are * bim], axis=1), None

    total, _ = lax.scan(one_window, jnp.zeros((pairs.shape[0], 2 * NB), F32), raw_blocks)
    return jnp.sum(spread(total, "tm"), axis=0) / (windows * lax.axis_size("tm"))


def local(raw_blocks, fir_taps, recorder_channel, pairs):
    windows, rows, length = raw_blocks.shape
    pair_count = pairs.shape[0]
    side, groups, team = 4, 16, 8
    share = pair_count // team
    table = jnp.asarray(table_values(length, 128))
    hbm = pl.BlockSpec(memory_space=pltpu.HBM)
    vmem = pl.BlockSpec(memory_space=pltpu.VMEM)
    dma = pltpu.SemaphoreType.DMA
    out, flag = pl.pallas_call(
        kernel,
        out_shape=[
            jax.ShapeDtypeStruct((pair_count, 2 * NB), BF16),
            jax.ShapeDtypeStruct((1,), F32),
        ],
        in_specs=[hbm] * 5,
        out_specs=[vmem, pl.BlockSpec(memory_space=pltpu.SMEM)],
        scratch_shapes=[
            pltpu.VMEM((windows, rows, length), BF16),
            pltpu.VMEM((1, 128), BF16),
            pltpu.VMEM((80, 128), jnp.int32),
            pltpu.VMEM((2, pair_count), jnp.int32),
            pltpu.VMEM((length + 128, 2 * NB), BF16),
            pltpu.VMEM((length, 2 * NB), BF16),
            pltpu.VMEM((2, rows, windows * NB), BF16),
            pltpu.VMEM((2, groups, 8, 128), F32),
            pltpu.VMEM((2, side, side, 8, 128), F32),
            pltpu.VMEM((2, side, 8, 128), F32),
            pltpu.VMEM((2, side, 8, 128), F32),
            pltpu.VMEM((2 * groups * 8, 128), F32),
            pltpu.VMEM((2 * groups * 8, 128), F32),
            pltpu.VMEM((2 * side * 8, 128), F32),
            pltpu.VMEM((2 * side * 8, 128), F32),
            pltpu.VMEM((2, side * CAP1, rows), BF16),
            pltpu.VMEM((2, side, side * CAP2, CAP1), BF16),
            pltpu.VMEM((2, 2, side, CAP1, 2 * NB), BF16),
            pltpu.VMEM((2, 2, side, CAP1, 2 * NB), BF16),
            pltpu.VMEM((2, 2, side, CAP2, 2 * NB), BF16),
            pltpu.VMEM((2, 2, side, SLOT, 2 * NB), BF16),
            pltpu.VMEM((2 * side, SLOT), F32),
            pltpu.VMEM((2, 2, pair_count, side * SLOT), BF16),
            pltpu.VMEM((2, team, share, NB), BF16),
            pltpu.VMEM((2, team, share, NB), BF16),
            pltpu.VMEM((2, team, share, NB), BF16),
            pltpu.VMEM((2, side, 8, 128), F32),
            dma((windows,)),
            dma((4,)),
            dma((2, side)),
            dma((2, side)),
            dma((2, side)),
            dma((2, side)),
            dma((2, 2, side)),
            dma((2, 2, side)),
            dma((2, 2, side)),
            dma((2, 2, side)),
            dma((2, team)),
            dma((2, team)),
            dma((2, team)),
            dma((2, team)),
            dma((2, side)),
            dma((2, side)),
        ],
        compiler_params=pltpu.CompilerParams(
            collective_id=0, has_side_effects=True, vmem_limit_bytes=40 * 2**20
        ),
    )(raw_blocks, fir_taps.reshape(1, -1), recorder_channel.reshape(-1, 128), pairs.T, table)
    return lax.cond(
        flag[0] > 0.0,
        lambda: general(raw_blocks, fir_taps, recorder_channel, pairs, table),
        lambda: out.astype(F32),
    )


def solution(mesh):
    in_specs = (P("tm", "chan", None), P(), P(), P("chan", None))
    out_specs = P("chan", None)
    return jax.shard_map(local, mesh=mesh, in_specs=in_specs, out_specs=out_specs, check_vma=False)
```
